128 devices in a mesh: ctx: 32 (over z, y, core), exp: 4 (over x).
Axes of the slice: x: 4, y: 4, z: 4, core: 2. Of those that a mesh axis runs over, the one named last changes fastest.
Arguments:
- projected: bfloat16 [3, 8192, 4096], P(None, 'ctx', 'exp'), may hold values from -6 to 6
- short_filter: float32 [3, 3, 4096], P(None, None, 'exp'), may hold values from -3.5 to 3.5
- long_filter: float32 [128, 4096], P(None, 'exp'), may hold values from -0.5 to 0.5
- residual_in: bfloat16 [8192, 4096], P('ctx', 'exp'), may hold values from -16 to 16
- norm_gain: float32 [4096], replicated, may hold values from 0.1 to 1.9
- expert_ids: int32 [8192], P('ctx'), may hold values from 0 to 15, as said below
- gate_weight: bfloat16 [32, 4096, 3072], P('ctx', None, 'exp'), may hold values from -0.09375 to 0.09375
- up_weight: bfloat16 [32, 4096, 3072], P('ctx', None, 'exp'), may hold values from -0.09375 to 0.09375
- down_weight: bfloat16 [32, 3072, 4096], P('ctx', 'exp'), may hold values from -0.078125 to 0.078125
Outputs:
- out: bfloat16 [8192, 4096], P('ctx', 'exp')
The draws below stay inside these ranges and needn't reach their ends.
Inputs may be any that keep to these rules, and one draw needn't show every extreme that they name: `expert_ids`: among the 256 positions of each device no expert is named more than 40 times; one expert, the same on all devices, is named exactly 40 times on every device.
All inputs are finite; a program needn't handle non-finite values.
Results may differ from the reference program's by a relative error of at most 0.008.
Values may be sent and summed in bfloat16 or wider, within the bound.
No kernel may reach another device: no remote copies, remote signals or barrier semaphores. Data moves between devices by JAX's collectives and lax.ppermute only.
A program may use at most 128 MiB of HBM per device.

```python
import jax
import jax.numpy as jnp
from jax import lax

D = 4096
FF = 6144
TAPS = 128
SHORT = 3
TOK_DEV = 256
TOKENS = 8192
EXPERTS = 16
CAP = 40
SLICE = 768


def draw_residual_in(key, part):
    key = jax.random.fold_in(key, 5)
    key_base, key_column, key_row = jax.random.split(key, 3)
    column = jnp.arange(D, dtype=jnp.float32) / (D - 1)
    base = jax.random.normal(key_base, (TOKENS, D), jnp.float32)
    ramp = 10.0 ** (0.5 * column - 0.25)
    jitter = jnp.exp(jax.random.uniform(key_column, (D,), jnp.float32, -0.2, 0.2))
    row_scale = 10.0 ** jax.random.uniform(key_row, (TOKENS, 1), jnp.float32, -0.5, 0.5)
    values = base * (ramp * jitter)[None, :] * row_scale
    return jnp.clip(values, -16.0, 16.0).astype(jnp.bfloat16)


def draw_expert_ids(key, part):
    key = jax.random.fold_in(key, 11)
    key_order, key_weights, key_shuffle = jax.random.split(key, 3)
    blocks = TOKENS // TOK_DEV
    remaining_rows = TOK_DEV - CAP
    order = jax.random.permutation(key_order, EXPERTS).astype(jnp.int32)
    weights = jax.random.randint(key_weights, (blocks, EXPERTS - 1), 2, 4).astype(jnp.int32)
    totals = jnp.sum(weights, axis=1, keepdims=True)
    counts = remaining_rows * weights // totals
    leftover = remaining_rows - jnp.sum(counts, axis=1, keepdims=True)
    counts = counts + (jnp.arange(EXPERTS - 1, dtype=jnp.int32)[None, :] < leftover).astype(jnp.int32)
    counts = jnp.concatenate([jnp.full((blocks, 1), CAP, jnp.int32), counts], axis=1)
    ends = jnp.cumsum(counts, axis=1)
    slots = jnp.arange(TOK_DEV, dtype=jnp.int32)
    ranks = jnp.sum((slots[None, :, None] >= ends[:, None, :]).astype(jnp.int32), axis=2)
    labels = order[ranks]
    keys = jax.random.split(key_shuffle, blocks)

    def permuted_row(row_key, row):
        return row[jax.random.permutation(row_key, TOK_DEV)]
    shuffled = jax.vmap(permuted_row)(keys, labels)
    return shuffled.reshape(TOKENS).astype(jnp.int32)


def shard_levels(key, dims, shards, smallest, high):
    gain = 1.0
    for axis_at, shards_of in shards:
        draws = jax.random.uniform(jax.random.fold_in(jax.random.fold_in(key, 6), axis_at), (shards_of,), jnp.float32, smallest / len(shards), high / len(shards))
        gain = gain * jnp.repeat(jnp.exp(draws), dims[axis_at] // shards_of).reshape((-1,) + (1,) * (len(dims) - 1 - axis_at))
    return gain


def bell_draw(rng, extent, spread, most, cuts=(), kind=jnp.bfloat16):
    factor_of = shard_levels(rng, extent, cuts, -0.22, 0.18) if cuts else 1.0
    entries = jax.random.normal(rng, extent, jnp.float32) * spread * factor_of
    return jnp.minimum(jnp.maximum(entries, -most), most).astype(kind)


def setup_inputs(seed: int = 0) -> dict:
    seeds = jax.random.split(jax.random.key(seed), 10)
    projected = bell_draw(seeds[0], (3, TOKENS, D), 1.0, 6.0, ((1, 32), (2, 4)))
    short_filter = bell_draw(seeds[1], (3, SHORT, D), SHORT ** -0.5, 3.5, ((2, 4),), jnp.float32)
    long_filter = bell_draw(seeds[2], (TAPS, D), TAPS ** -0.5, 0.5, ((1, 4),), jnp.float32)
    residual_in = draw_residual_in(jax.random.fold_in(seeds[9], 71), 0)
    norm_gain = jnp.clip(1.0 + 0.18 * jax.random.normal(seeds[4], (D,), jnp.float32), 0.1, 1.9)
    expert_ids = draw_expert_ids(jax.random.fold_in(seeds[9], 71), 0)
    gate_weight = bell_draw(seeds[6], (2 * EXPERTS, D, FF // 2), D ** -0.5, 0.09375, ((0, 32), (2, 4)))
    up_weight = bell_draw(seeds[7], (2 * EXPERTS, D, FF // 2), D ** -0.5, 0.09375, ((0, 32), (2, 4)))
    down_weight = bell_draw(seeds[8], (2 * EXPERTS, FF // 2, D), FF ** -0.5, 0.078125, ((0, 32), (1, 4)))
    return dict(projected=projected, short_filter=short_filter, long_filter=long_filter, residual_in=residual_in, norm_gain=norm_gain, expert_ids=expert_ids, gate_weight=gate_weight, up_weight=up_weight, down_weight=down_weight)


def short_conv(field, kernel):
    values = field.astype(jnp.float32)
    padded = jnp.pad(values, ((SHORT - 1, 0), (0, 0)))
    length = values.shape[0]
    total = jnp.zeros_like(values)
    for offset in range(SHORT):
        total = total + kernel[offset] * padded[SHORT - 1 - offset:SHORT - 1 - offset + length]
    return total

def long_conv(product, long_filter):
    padded = jnp.pad(product.astype(jnp.float32), ((TAPS - 1, 0), (0, 0)))

    def add_tap(offset, total):
        window = lax.dynamic_slice_in_dim(padded, TAPS - 1 - offset, TOKENS, 0)
        return total + long_filter[offset] * window
    return lax.fori_loop(0, TAPS, add_tap, jnp.zeros((TOKENS, D), jnp.float32))

def expert_rows(rows_in, expert, gate_weight, up_weight, down_weight):
    count = rows_in.shape[0]
    total = jnp.zeros((count, D), jnp.float32)
    for half in range(2):
        index = 2 * expert + half
        w_gate = lax.dynamic_index_in_dim(gate_weight, index, 0, keepdims=False)
        w_up = lax.dynamic_index_in_dim(up_weight, index, 0, keepdims=False)
        w_down = lax.dynamic_index_in_dim(down_weight, index, 0, keepdims=False)
        gate_pre = jnp.dot(rows_in, w_gate, preferred_element_type=jnp.float32)
        up_pre = jnp.dot(rows_in, w_up, preferred_element_type=jnp.float32)
        hidden = (jax.nn.silu(gate_pre) * up_pre).astype(jnp.bfloat16)
        hidden_block_list = hidden.reshape(count, FF // 2 // SLICE, SLICE).astype(jnp.float32)
        down_block_list = w_down.reshape(FF // 2 // SLICE, SLICE, D).astype(jnp.float32)
        partition_list = jnp.einsum('thy,hym->thm', hidden_block_list, down_block_list, precision=lax.Precision.HIGHEST)
        rounded = lax.optimization_barrier(partition_list.astype(jnp.bfloat16)).astype(jnp.float32)
        total = total + lax.optimization_barrier(jnp.sum(rounded, axis=1))
    return total

def reference(projected, short_filter, long_filter, residual_in, norm_gain, expert_ids, gate_weight, up_weight, down_weight):
    query_s = short_conv(projected[0], short_filter[0])
    key_s = short_conv(projected[1], short_filter[1])
    value_s = short_conv(projected[2], short_filter[2])
    product = (key_s * value_s).astype(jnp.bfloat16)
    long_out = long_conv(product, long_filter)
    h_state = (residual_in.astype(jnp.float32) + query_s * long_out).astype(jnp.bfloat16)
    h_float = h_state.astype(jnp.float32)
    scale = lax.rsqrt(lax.optimization_barrier(jnp.mean(h_float * h_float, axis=1, keepdims=True)) + 1e-06)
    normed = (h_float * scale * norm_gain[None, :]).astype(jnp.bfloat16)
    piece_rows = 64
    order = jnp.argsort(expert_ids, stable=True).astype(jnp.int32)
    sorted_ids = expert_ids[order].astype(jnp.int32)
    counts = lax.optimization_barrier(jnp.sum((expert_ids[:, None] == jnp.arange(EXPERTS, dtype=jnp.int32)[None, :]).astype(jnp.int32), axis=0))
    expert_starts = (jnp.cumsum(counts) - counts).astype(jnp.int32)
    block_starts = jnp.arange(0, TOKENS, piece_rows, dtype=jnp.int32)
    cuts = jnp.sort(jnp.concatenate([block_starts, expert_starts, jnp.array([TOKENS], dtype=jnp.int32)]))
    pieces = cuts.shape[0] - 1
    sorted_rows = jnp.concatenate([normed[order], jnp.zeros((piece_rows, D), jnp.bfloat16)], axis=0)
    padded_expert_indices = jnp.concatenate([sorted_ids, jnp.zeros((1,), jnp.int32)])

    def add_piece(index, accum):
        start = cuts[index]
        stop = cuts[index + 1]
        expert = padded_expert_indices[start]
        rows_in = lax.dynamic_slice_in_dim(sorted_rows, start, piece_rows, 0)
        result = expert_rows(rows_in, expert, gate_weight, up_weight, down_weight)
        keep = (jnp.arange(piece_rows, dtype=jnp.int32) < stop - start)[:, None]
        current = lax.dynamic_slice_in_dim(accum, start, piece_rows, 0)
        return lax.dynamic_update_slice_in_dim(accum, current + jnp.where(keep, result, jnp.zeros_like(result)), start, 0)
    accum = lax.fori_loop(0, pieces, add_piece, jnp.zeros((TOKENS + piece_rows, D), jnp.float32))
    moe = jnp.zeros((TOKENS, D), jnp.float32).at[order].set(accum[:TOKENS])
    return (h_float + moe).astype(jnp.bfloat16)
```

```python
import functools

import jax
import jax.numpy as jnp
import numpy as np
from jax import lax
from jax.experimental import pallas as pl
from jax.experimental.pallas import tpu as pltpu
from jax.sharding import Mesh
from jax.sharding import PartitionSpec as P

D = 4096
TAPS = 128
TOK = 256
QUARTER = 1024
HID = 768
EXPERTS = 16
CAP = 40
SLOTS = EXPERTS * CAP
SPAN = TOK + TAPS
BINS = 200
HALO = 144
QHALO = 16
LANES = 256
HALF = 320
ROWS = 2 * HALF
VMEM = 100 << 19


def dft_matrices():
    n = np.arange(SPAN)
    k = np.arange(BINS)
    angle = 2 * np.pi * ((k[:, None] * n[None, :]) % SPAN) / SPAN
    live = (k <= SPAN // 2)[:, None]
    forward = np.concatenate([np.cos(angle) * live, -np.sin(angle) * live], axis=0)
    weight = np.where((k == 0) | (k == SPAN // 2), 1.0, 2.0) * (k <= SPAN // 2) / SPAN
    back = np.concatenate(
        [np.cos(angle).T[TAPS:] * weight, -np.sin(angle).T[TAPS:] * weight], axis=1
    )
    return forward.astype(np.float32), back.astype(np.float32)


def split(value, parts):
    out = []
    rest = value
    for _ in range(parts):
        piece = rest.astype(jnp.bfloat16)
        out.append(piece)
        rest = rest - piece.astype(jnp.float32)
    return out


def split_np(value, parts):
    out = []
    rest = value
    for _ in range(parts):
        piece = rest.astype(jnp.bfloat16)
        out.append(piece)
        rest = rest - piece.astype(np.float32)
    return out


def mm(a, b):
    return jnp.dot(a, b, preferred_element_type=jnp.float32)


def slots_of(ids_col, ids_row, axis):
    first = lax.broadcasted_iota(jnp.int32, (TOK, TOK), 0)
    second = lax.broadcasted_iota(jnp.int32, (TOK, TOK), 1)
    same = ids_col == ids_row
    earlier = (first < second) if axis == 0 else (second < first)
    rank = jnp.sum(jnp.where(same & earlier, 1.0, 0.0), axis=axis, keepdims=True)
    ids = ids_row if axis == 0 else ids_col
    return ids * CAP + rank.astype(jnp.int32)


def taps3(ext, filt, start, length):
    return (
        filt[0:1] * ext[start : start + length]
        + filt[1:2] * ext[start - 1 : start - 1 + length]
        + filt[2:3] * ext[start - 2 : start - 2 + length]
    )


def front_kernel(
    x_ref, proj, halo_kv, halo_q, short, long_f, res, gain, ids_col, ids_row,
    fwd1, fwd2, fwd3, back1, back2, back3, h_out, send_out,
):
    f32 = jnp.float32

    def extended(halo, body):
        return jnp.concatenate([halo.astype(f32), body.astype(f32)], axis=0)

    s1 = taps3(extended(halo_kv[0], proj[1]), short[1], HALO - TAPS, SPAN)
    s2 = taps3(extended(halo_kv[1], proj[2]), short[2], HALO - TAPS, SPAN)
    s0 = taps3(extended(halo_q[...], proj[0]), short[0], QHALO, TOK)
    kv = (s1 * s2).astype(jnp.bfloat16)
    spec = mm(fwd1[...], kv) + mm(fwd2[...], kv) + mm(fwd3[...], kv)
    f1, f2, f3 = split(long_f[...], 3)
    a1, a2, a3 = fwd1[:, :TAPS], fwd2[:, :TAPS], fwd3[:, :TAPS]
    filt = mm(a1, f1) + (mm(a1, f2) + mm(a2, f1)) + (mm(a1, f3) + mm(a2, f2) + mm(a3, f1))
    re, im = spec[:BINS], spec[BINS:]
    fre, fim = filt[:BINS], filt[BINS:]
    prod = jnp.concatenate([re * fre - im * fim, re * fim + im * fre], axis=0)
    p1, p2, p3 = split(prod, 3)
    b1, b2, b3 = back1[...], back2[...], back3[...]
    long_out = mm(b1, p1) + (mm(b1, p2) + mm(b2, p1)) + (mm(b1, p3) + mm(b2, p2) + mm(b3, p1))
    h = (res[...].astype(f32) + s0 * long_out).astype(jnp.bfloat16)
    h_out[...] = h
    gained = (h.astype(f32) * gain[...]).astype(jnp.bfloat16)
    slot_row = slots_of(ids_col[...], ids_row[...], 0)
    slot = lax.broadcasted_iota(jnp.int32, (SLOTS, TOK), 0)
    pick = jnp.where(slot == slot_row, 1.0, 0.0).astype(jnp.bfloat16)
    send_out[...] = mm(pick, gained).astype(jnp.bfloat16)


def front(x_at, projected, halo_kv, halo_q, short, long_f, res, gain, ids):
    forward, back = dft_matrices()
    fwd = [jnp.asarray(p) for p in split_np(forward, 3)]
    bck = [jnp.asarray(p) for p in split_np(back, 3)]
    steps = QUARTER // LANES

    def whole(shape):
        return pl.BlockSpec(shape, lambda i, x: (0,) * len(shape))

    in_specs = [
        pl.BlockSpec((3, TOK, LANES), lambda i, x: (0, 0, i)),
        pl.BlockSpec((2, HALO, LANES), lambda i, x: (0, 0, i)),
        pl.BlockSpec((QHALO, LANES), lambda i, x: (0, i)),
        pl.BlockSpec((3, 3, LANES), lambda i, x: (0, 0, i)),
        pl.BlockSpec((TAPS, LANES), lambda i, x: (0, i)),
        pl.BlockSpec((TOK, LANES), lambda i, x: (0, i)),
        pl.BlockSpec((1, LANES), lambda i, x: (0, x[0] * steps + i)),
        whole((TOK, 1)),
        whole((1, TOK)),
    ]
    in_specs += [whole((2 * BINS, SPAN))] * 3 + [whole((TOK, 2 * BINS))] * 3
    return pl.pallas_call(
        front_kernel,
        grid_spec=pltpu.PrefetchScalarGridSpec(
            num_scalar_prefetch=1,
            grid=(steps,),
            in_specs=in_specs,
            out_specs=[
                pl.BlockSpec((TOK, LANES), lambda i, x: (0, i)),
                pl.BlockSpec((SLOTS, LANES), lambda i, x: (0, i)),
            ],
        ),
        out_shape=[
            jax.ShapeDtypeStruct((TOK, QUARTER), jnp.bfloat16),
            jax.ShapeDtypeStruct((SLOTS, QUARTER), jnp.bfloat16),
        ],
        compiler_params=pltpu.CompilerParams(vmem_limit_bytes=VMEM),
        name="front",
    )(
        x_at, projected, halo_kv, halo_q, short, long_f, res, gain.reshape(1, D),
        ids.reshape(TOK, 1), ids.reshape(1, TOK), *fwd, *bck,
    )


PIECES = ((0, 0, HALF), (1, 0, HALF), (2, 0, HALF), (3, 0, HALF // 2), (3, HALF // 2, HALF // 2))


def expert_kernel(x_ref, *refs):
    pieces = refs[:10]
    wg, wu, wd, ig, own_out, sib_out, xs, accg, accu, ssq, hid, sems = refs[10:]
    i = pl.program_id(0)
    copies = []
    for core in range(2):
        for n, (block, start, rows) in enumerate(PIECES):
            at = core * 5 + n
            copies.append(
                (
                    block,
                    pltpu.make_async_copy(
                        pieces[at],
                        xs.at[block, pl.ds(core * HALF + start, rows)],
                        sems.at[at],
                    ),
                )
            )

    @pl.when(i == 0)
    def _():
        for _, copy in sorted(copies, key=lambda c: c[0]):
            copy.start()

    for k in range(4):

        @pl.when(i == k)
        def _():
            for block, copy in copies:
                if block == k:
                    copy.wait()
            xk = xs[k]
            g = mm(xk, wg[...])
            u = mm(xk, wu[...])
            h = xk.astype(jnp.float32) * ig[0]
            sq = h * h
            part = sq[:, 0:128]
            for c in range(1, QUARTER // 128):
                part = part + sq[:, c * 128 : (c + 1) * 128]
            if k == 0:
                accg[...] = g
                accu[...] = u
                ssq[...] = part
            elif k < 3:
                accg[...] += g
                accu[...] += u
                ssq[...] += part
            else:
                total = jnp.sum(ssq[...] + part, axis=1, keepdims=True)
                scale = lax.rsqrt(total / D + 1e-06)
                gate = (accg[...] + g) * scale
                up = (accu[...] + u) * scale
                hid[...] = (gate / (1.0 + jnp.exp(-gate)) * up).astype(jnp.bfloat16)

    @pl.when(i >= 4)
    def _():
        y = mm(hid[...], wd[...]).astype(jnp.bfloat16)
        own_out[0] = y[:HALF]
        sib_out[0] = y[HALF:]


def expert(x_at, pieces, wg, wu, wd, inv_gain):
    def k_block(i, x):
        k = jnp.minimum(i, 3)
        off = jnp.where(k == 1, 3, jnp.where(k == 0, 0, k - 1))
        return lax.rem(x[0] + off, 4)

    def n_block(i, x):
        j = jnp.maximum(i - 4, 0)
        off = jnp.where(j == 0, 2, jnp.where(j == 1, 1, jnp.where(j == 2, 3, 0)))
        return lax.rem(x[0] + off, 4)

    any_spec = pl.BlockSpec(memory_space=pl.ANY)
    out_spec = pl.BlockSpec((1, HALF, QUARTER), lambda i, x: (jnp.maximum(i - 4, 0), 0, 0))
    out_type = jax.ShapeDtypeStruct((4, HALF, QUARTER), jnp.bfloat16)
    return pl.pallas_call(
        expert_kernel,
        grid_spec=pltpu.PrefetchScalarGridSpec(
            num_scalar_prefetch=1,
            grid=(8,),
            in_specs=[any_spec] * 10
            + [
                pl.BlockSpec((QUARTER, HID), lambda i, x: (k_block(i, x), 0)),
                pl.BlockSpec((QUARTER, HID), lambda i, x: (k_block(i, x), 0)),
                pl.BlockSpec((HID, QUARTER), lambda i, x: (0, n_block(i, x))),
                pl.BlockSpec((1, 1, QUARTER), lambda i, x: (k_block(i, x), 0, 0)),
            ],
            out_specs=[out_spec, out_spec],
            scratch_shapes=[
                pltpu.VMEM((4, ROWS, QUARTER), jnp.bfloat16),
                pltpu.VMEM((ROWS, HID), jnp.float32),
                pltpu.VMEM((ROWS, HID), jnp.float32),
                pltpu.VMEM((ROWS, 128), jnp.float32),
                pltpu.VMEM((ROWS, HID), jnp.bfloat16),
                pltpu.SemaphoreType.DMA((10,)),
            ],
        ),
        out_shape=[out_type, out_type],
        compiler_params=pltpu.CompilerParams(vmem_limit_bytes=VMEM),
        cost_estimate=pl.CostEstimate(
            flops=2 * 3 * ROWS * D * HID, bytes_accessed=32 << 20, transcendentals=ROWS * HID
        ),
        name="expert",
    )(x_at, *pieces, wg, wu, wd, inv_gain)


def finish_kernel(h, back, ids_col, ids_row, out):
    slot_col = slots_of(ids_col[...], ids_row[...], 1)
    slot = lax.broadcasted_iota(jnp.int32, (TOK, SLOTS), 1)
    pick = jnp.where(slot == slot_col, 1.0, 0.0).astype(jnp.bfloat16)
    moe = mm(pick, back[...])
    out[...] = (h[...].astype(jnp.float32) + moe).astype(jnp.bfloat16)


def finish(h, back, ids):
    return pl.pallas_call(
        finish_kernel,
        grid=(QUARTER // LANES,),
        in_specs=[
            pl.BlockSpec((TOK, LANES), lambda i: (0, i)),
            pl.BlockSpec((SLOTS, LANES), lambda i: (0, i)),
            pl.BlockSpec((TOK, 1), lambda i: (0, 0)),
            pl.BlockSpec((1, TOK), lambda i: (0, 0)),
        ],
        out_specs=pl.BlockSpec((TOK, LANES), lambda i: (0, i)),
        out_shape=jax.ShapeDtypeStruct((TOK, QUARTER), jnp.bfloat16),
        compiler_params=pltpu.CompilerParams(vmem_limit_bytes=VMEM),
        name="finish",
    )(h, back, ids.reshape(TOK, 1), ids.reshape(1, TOK))


def along_x(block, step):
    return lax.ppermute(block, "x", [(i, (i + step) % 4) for i in range(4)])


def other_core(block):
    return lax.ppermute(block, "c", [(0, 1), (1, 0)])


def add(*terms):
    total = terms[0].astype(jnp.float32)
    for term in terms[1:]:
        total = total + term.astype(jnp.float32)
    return total.astype(jnp.bfloat16)


def gather_x(own):
    mid = HALF // 2
    left = along_x(own, 1)
    right = along_x(own, -1)
    far_a = along_x(left[:mid], 1)
    far_b = along_x(right[mid:], -1)
    mine = [own, left, right, far_a, far_b]
    return mine + [other_core(piece) for piece in mine]


def scatter_x(own_out, sib_out):
    mid = HALF // 2
    far, right, left, here = [add(own_out[j], other_core(sib_out[j])) for j in range(4)]
    via_left = along_x(far[:mid], 1)
    via_right = along_x(far[mid:], -1)
    to_right = jnp.concatenate([add(right[:mid], via_left), right[mid:]], axis=0)
    to_left = jnp.concatenate([left[:mid], add(left[mid:], via_right)], axis=0)
    from_left = along_x(to_right, 1)
    from_right = along_x(to_left, -1)
    return add(here, from_left, from_right)


def body(
    projected, short_filter, long_filter, residual_in, norm_gain, expert_ids,
    gate_weight, up_weight, down_weight,
):
    x_at = lax.axis_index("x").astype(jnp.int32).reshape(1)
    route = [(i, i + 1) for i in range(31)]
    halo_kv = lax.ppermute(projected[1:, TOK - HALO :, :], ("z", "y", "c"), route)
    halo_q = lax.ppermute(projected[0, TOK - QHALO :, :], ("z", "y", "c"), route)
    h, send = front(
        x_at, projected, halo_kv, halo_q, short_filter, long_filter, residual_in,
        norm_gain, expert_ids,
    )
    got = lax.all_to_all(
        send.reshape(EXPERTS, CAP, QUARTER), ("z", "y"), split_axis=0, concat_axis=0, tiled=True
    ).reshape(SLOTS, QUARTER)
    inv_gain = (1.0 / norm_gain).reshape(4, 1, QUARTER)
    weights = (gate_weight[0], up_weight[0], down_weight[0])
    done = []
    for part in range(2):
        pieces = gather_x(got[part * HALF : (part + 1) * HALF])
        own_out, sib_out = expert(x_at, pieces, *weights, inv_gain)
        done.append(scatter_x(own_out, sib_out))
    back = lax.all_to_all(
        jnp.concatenate(done, axis=0).reshape(EXPERTS, CAP, QUARTER),
        ("z", "y"), split_axis=0, concat_axis=0, tiled=True,
    ).reshape(SLOTS, QUARTER)
    return finish(h, back, expert_ids)


def solution(mesh):
    grid = Mesh(mesh.devices.reshape(4, 4, 2, 4), ("z", "y", "c", "x"))
    ctx = ("z", "y", "c")
    return jax.shard_map(
        body,
        mesh=grid,
        in_specs=(
            P(None, ctx, "x"),
            P(None, None, "x"),
            P(None, "x"),
            P(ctx, "x"),
            P(),
            P(ctx),
            P(ctx, None, "x"),
            P(ctx, None, "x"),
            P(ctx, "x", None),
        ),
        out_specs=P(ctx, "x"),
        check_vma=False,
    )
```

```python
import jax
import jax.numpy as jnp
import numpy as np
from jax import lax
from jax.experimental import pallas as pl
from jax.experimental.pallas import tpu as pltpu
from jax.sharding import Mesh
from jax.sharding import PartitionSpec as P

D = 4096
TAPS = 128
TOK = 256
QUARTER = 1024
HID = 768
EXPERTS = 16
CAP = 40
SLOTS = EXPERTS * CAP
SPAN = TOK + TAPS
BINS = 200
HALO = 144
QHALO = 16
LANES = 256
HALF = 320
ROWS = 2 * HALF


def dft_matrices():
    n = np.arange(SPAN)
    k = np.arange(BINS)
    angle = 2 * np.pi * ((k[:, None] * n[None, :]) % SPAN) / SPAN
    live = (k <= SPAN // 2)[:, None]
    forward = np.concatenate([np.cos(angle) * live, -np.sin(angle) * live], axis=0)
    weight = np.where((k == 0) | (k == SPAN // 2), 1.0, 2.0) * (k <= SPAN // 2) / SPAN
    back = np.concatenate(
        [np.cos(angle).T[TAPS:] * weight, -np.sin(angle).T[TAPS:] * weight], axis=1
    )
    return split_np(forward.astype(np.float32)), split_np(back.astype(np.float32))


def split_np(value):
    high = value.astype(jnp.bfloat16)
    low = (value - high.astype(np.float32)).astype(jnp.bfloat16)
    return np.stack([high, low])


def split(value):
    high = value.astype(jnp.bfloat16)
    return high, (value - high.astype(jnp.float32)).astype(jnp.bfloat16)


def mm(a, b):
    return jnp.dot(a, b, preferred_element_type=jnp.float32)


def mm_split(a, b):
    high, low = split(b)
    return mm(a[0], high) + (mm(a[0], low) + mm(a[1], high))


def slots_of(ids_col, ids_row, axis):
    first = lax.broadcasted_iota(jnp.int32, (TOK, TOK), 0)
    second = lax.broadcasted_iota(jnp.int32, (TOK, TOK), 1)
    same = ids_col == ids_row
    earlier = (first < second) if axis == 0 else (second < first)
    rank = jnp.sum(jnp.where(same & earlier, 1.0, 0.0), axis=axis, keepdims=True)
    ids = ids_row if axis == 0 else ids_col
    return ids * CAP + rank.astype(jnp.int32)


def taps3(ext, filt, start, length):
    return (
        filt[0:1] * ext[start : start + length]
        + filt[1:2] * ext[start - 1 : start - 1 + length]
        + filt[2:3] * ext[start - 2 : start - 2 + length]
    )


def spectrum_kernel(proj, short, long_f, fwd, spec_out, filt_out, table, sem):
    copy = pltpu.make_async_copy(fwd, table, sem)

    @pl.when(pl.program_id(0) == 0)
    def _():
        copy.start()

    zeros = jnp.zeros((8, LANES), jnp.float32)

    def filtered(f):
        ext = jnp.concatenate([zeros, proj[f].astype(jnp.float32)], axis=0)
        return taps3(ext, short[f], 8, TOK)

    live = lax.broadcasted_iota(jnp.int32, (TOK, LANES), 0) >= 2
    kv = jnp.where(live, filtered(1) * filtered(2), 0.0).astype(jnp.bfloat16)

    @pl.when(pl.program_id(0) == 0)
    def _():
        copy.wait()

    filt_out[...] = mm_split((table[0, :, :TAPS], table[1, :, :TAPS]), long_f[...])
    spec_out[...] = mm(table[0, :, TAPS:], kv) + mm(table[1, :, TAPS:], kv)


def spectrum(projected, short, long_f, fwd):
    steps = QUARTER // LANES
    return pl.pallas_call(
        spectrum_kernel,
        grid=(steps,),
        in_specs=[
            pl.BlockSpec((3, TOK, LANES), lambda i: (0, 0, i)),
            pl.BlockSpec((3, 3, LANES), lambda i: (0, 0, i)),
            pl.BlockSpec((TAPS, LANES), lambda i: (0, i)),
            pl.BlockSpec(memory_space=pltpu.HBM),
        ],
        out_specs=[pl.BlockSpec((2 * BINS, LANES), lambda i: (0, i))] * 2,
        out_shape=[jax.ShapeDtypeStruct((2 * BINS, QUARTER), jnp.float32)] * 2,
        scratch_shapes=[
            pltpu.VMEM((2, 2 * BINS, SPAN), jnp.bfloat16),
            pltpu.SemaphoreType.DMA,
        ],
        compiler_params=pltpu.CompilerParams(vmem_limit_bytes=60 << 20),
        cost_estimate=pl.CostEstimate(
            flops=4 << 30, bytes_accessed=8 << 20, transcendentals=0
        ),
        name="spectrum",
    )(projected, short, long_f, fwd)


def front_kernel(
    x_ref, proj, halo, short, spec, filt, res, gain, ids_col, ids_row,
    fwd, back, h_out, send_out, fwd_table, back_table, sems,
):
    f32 = jnp.float32
    copies = [
        pltpu.make_async_copy(fwd, fwd_table, sems.at[0]),
        pltpu.make_async_copy(back, back_table, sems.at[1]),
    ]

    @pl.when(pl.program_id(0) == 0)
    def _():
        for copy in copies:
            copy.start()

    def filtered(f):
        ext = jnp.concatenate([halo[(f - 1) * HALO : f * HALO], proj[f, :QHALO]], axis=0).astype(f32)
        return taps3(ext, short[f], HALO - TAPS, HALO)

    live = lax.broadcasted_iota(jnp.int32, (HALO, LANES), 0) < TAPS + 2
    kv = jnp.where(live, filtered(1) * filtered(2), 0.0).astype(jnp.bfloat16)
    ext = jnp.concatenate([halo[2 * HALO :], proj[0]], axis=0).astype(f32)
    s0 = taps3(ext, short[0], QHALO, TOK)

    @pl.when(pl.program_id(0) == 0)
    def _():
        for copy in copies:
            copy.wait()

    total = spec[...] + mm(fwd_table[0, :, :HALO], kv) + mm(fwd_table[1, :, :HALO], kv)
    re, im = total[:BINS], total[BINS:]
    fre, fim = filt[:BINS], filt[BINS:]
    prod = jnp.concatenate([re * fre - im * fim, re * fim + im * fre], axis=0)
    long_out = mm_split((back_table[0], back_table[1]), prod)
    h = (res[...].astype(f32) + s0 * long_out).astype(jnp.bfloat16)
    h_out[...] = h
    gained = (h.astype(f32) * gain[...]).astype(jnp.bfloat16)
    slot_row = slots_of(ids_col[...], ids_row[...], 0)
    slot = lax.broadcasted_iota(jnp.int32, (SLOTS, TOK), 0)
    pick = jnp.where(slot == slot_row, 1.0, 0.0).astype(jnp.bfloat16)
    send_out[...] = mm(pick, gained).astype(jnp.bfloat16)


def front(x_at, projected, halo, short, spec, filt, res, gain, ids, fwd, back):
    steps = QUARTER // LANES

    def whole(shape):
        return pl.BlockSpec(shape, lambda i, x: (0,) * len(shape))

    def columns(rows):
        return pl.BlockSpec((rows, LANES), lambda i, x: (0, i))

    return pl.pallas_call(
        front_kernel,
        grid_spec=pltpu.PrefetchScalarGridSpec(
            num_scalar_prefetch=1,
            grid=(steps,),
            in_specs=[
                pl.BlockSpec((3, TOK, LANES), lambda i, x: (0, 0, i)),
                columns(2 * HALO + QHALO),
                pl.BlockSpec((3, 3, LANES), lambda i, x: (0, 0, i)),
                columns(2 * BINS),
                columns(2 * BINS),
                columns(TOK),
                pl.BlockSpec((1, LANES), lambda i, x: (0, x[0] * steps + i)),
                whole((TOK, 1)),
                whole((1, TOK)),
                pl.BlockSpec(memory_space=pltpu.HBM),
                pl.BlockSpec(memory_space=pltpu.HBM),
            ],
            out_specs=[columns(TOK), columns(SLOTS)],
            scratch_shapes=[
                pltpu.VMEM((2, 2 * BINS, SPAN), jnp.bfloat16),
                pltpu.VMEM((2, TOK, 2 * BINS), jnp.bfloat16),
                pltpu.SemaphoreType.DMA((2,)),
            ],
        ),
        out_shape=[
            jax.ShapeDtypeStruct((TOK, QUARTER), jnp.bfloat16),
            jax.ShapeDtypeStruct((SLOTS, QUARTER), jnp.bfloat16),
        ],
        compiler_params=pltpu.CompilerParams(vmem_limit_bytes=60 << 20),
        name="front",
    )(
        x_at, projected, halo, short, spec, filt, res, gain.reshape(1, D),
        ids.reshape(TOK, 1), ids.reshape(1, TOK), fwd, back,
    )


MID = HALF // 2
K_OFFSET = (0, 3, 1, 2)
N_OFFSET = (2, 1, 3, 0)
EXPERT_VMEM = 50 << 20


def aligned(q):
    return pl.ds(pl.multiple_of(q * QUARTER, QUARTER), QUARTER)


def x_copy(piece, xs, block, core, start, sem):
    return pltpu.make_async_copy(
        piece, xs.at[block, pl.ds(core * HALF + start, piece.shape[0])], sem
    )


def add_squares(squares, xk, ig):
    h = xk.astype(jnp.float32) * ig
    sq = h * h
    for c in range(QUARTER // 128):
        squares = squares + sq[:, c * 128 : (c + 1) * 128]
    return squares


def near_kernel(x_ref, *refs):
    pieces = refs[:6]
    wg, wu, ig, g_out, u_out, sq_out, xs, wgs, wus, accg, accu, x_sem, w_sem, y_sem = refs[6:]
    k_at = [lax.rem(x_ref[0] + K_OFFSET[k], 4) for k in range(3)]
    copies = []
    for k in range(3):
        copies.append(
            [
                x_copy(pieces[k], xs, k, 0, 0, x_sem.at[k]),
                x_copy(pieces[3 + k], xs, k, 1, 0, x_sem.at[3 + k]),
                pltpu.make_async_copy(wg.at[aligned(k_at[k])], wgs.at[k], w_sem.at[0, k]),
                pltpu.make_async_copy(wu.at[aligned(k_at[k])], wus.at[k], w_sem.at[1, k]),
            ]
        )
        for copy in copies[k]:
            copy.start()
    squares = jnp.zeros((ROWS, 128), jnp.float32)
    for k in range(3):
        for copy in copies[k]:
            copy.wait()
        g = mm(xs[k], wgs[k])
        u = mm(xs[k], wus[k])
        squares = add_squares(squares, xs[k], ig[k_at[k]])
        if k == 0:
            accg[...] = g
            accu[...] = u
        else:
            accg[...] += g
            accu[...] += u
    sq_out[...] = squares
    outs = [
        pltpu.make_async_copy(accg, g_out, y_sem.at[0]),
        pltpu.make_async_copy(accu, u_out, y_sem.at[1]),
    ]
    for copy in outs:
        copy.start()
    for copy in outs:
        copy.wait()


def near(x_at, pieces, wg, wu, inv_gain):
    any_spec = pl.BlockSpec(memory_space=pl.ANY)
    vmem_spec = pl.BlockSpec(memory_space=pltpu.VMEM)
    bf16, f32 = jnp.bfloat16, jnp.float32
    return pl.pallas_call(
        near_kernel,
        in_specs=[pl.BlockSpec(memory_space=pltpu.SMEM)] + [any_spec] * 8 + [vmem_spec],
        out_specs=[any_spec, any_spec, vmem_spec],
        out_shape=[
            jax.ShapeDtypeStruct((ROWS, HID), f32),
            jax.ShapeDtypeStruct((ROWS, HID), f32),
            jax.ShapeDtypeStruct((ROWS, 128), f32),
        ],
        scratch_shapes=[
            pltpu.VMEM((3, ROWS, QUARTER), bf16),
            pltpu.VMEM((3, QUARTER, HID), bf16),
            pltpu.VMEM((3, QUARTER, HID), bf16),
            pltpu.VMEM((ROWS, HID), f32),
            pltpu.VMEM((ROWS, HID), f32),
            pltpu.SemaphoreType.DMA((6,)),
            pltpu.SemaphoreType.DMA((2, 3)),
            pltpu.SemaphoreType.DMA((2,)),
        ],
        compiler_params=pltpu.CompilerParams(vmem_limit_bytes=EXPERT_VMEM),
        cost_estimate=pl.CostEstimate(
            flops=0, bytes_accessed=0, transcendentals=0
        ),
        name="near",
    )(x_at, *pieces, wg, wu, inv_gain)


def far_kernel(x_ref, *refs):
    pieces = refs[:4]
    g_in, u_in, sq_in, wg, wu, wd, ig = refs[4:11]
    outs = refs[11:19]
    xs, wgs, wus, wds, ys, accg, accu, hid, x_sem, w_sem, a_sem, y_sem = refs[19:]
    k_at = lax.rem(x_ref[0] + K_OFFSET[3], 4)
    first = [
        x_copy(pieces[n], xs, 0, n // 2, (n % 2) * MID, x_sem.at[n]) for n in range(4)
    ] + [
        pltpu.make_async_copy(wg.at[aligned(k_at)], wgs, w_sem.at[0]),
        pltpu.make_async_copy(wu.at[aligned(k_at)], wus, w_sem.at[1]),
    ]
    sums = [
        pltpu.make_async_copy(g_in, accg, a_sem.at[0]),
        pltpu.make_async_copy(u_in, accu, a_sem.at[1]),
    ]
    down = [
        pltpu.make_async_copy(
            wd.at[:, aligned(lax.rem(x_ref[0] + N_OFFSET[j], 4))], wds.at[j], w_sem.at[2 + j]
        )
        for j in range(4)
    ]
    for copy in first + sums + down:
        copy.start()

    places = {
        (0, 0): (0, 0), (0, 1): (1, 1), (1, 0): (2, 0), (1, 1): (0, 1),
        (2, 0): (1, 0), (2, 1): (2, 1), (3, 0): (3, 0), (3, 1): (3, 1),
    }
    results = [[] for _ in range(4)]
    for (j, half), (out, at) in places.items():
        for core in range(2):
            results[j].append(
                pltpu.make_async_copy(
                    ys.at[j, pl.ds(core * HALF + half * MID, MID)],
                    outs[core * 4 + out].at[pl.ds(at * MID, MID)],
                    y_sem.at[j, core * 2 + half],
                )
            )
    for copy in first:
        copy.wait()
    xk = xs[0]
    g = mm(xk, wgs[...])
    u = mm(xk, wus[...])
    squares = add_squares(sq_in[...], xk, ig[k_at])
    scale = lax.rsqrt(jnp.sum(squares, axis=1, keepdims=True) / D + 1e-06)
    for copy in sums:
        copy.wait()
    gate = (accg[...] + g) * scale
    up = (accu[...] + u) * scale
    hid[...] = (gate / (1.0 + jnp.exp(-gate)) * up).astype(jnp.bfloat16)
    for j in range(4):
        down[j].wait()
        ys[j] = mm(hid[...], wds[j]).astype(jnp.bfloat16)
        for copy in results[j]:
            copy.start()
    for j in range(4):
        for copy in results[j]:
            copy.wait()


def far(x_at, pieces, sums, wg, wu, wd, inv_gain):
    any_spec = pl.BlockSpec(memory_space=pl.ANY)
    vmem_spec = pl.BlockSpec(memory_space=pltpu.VMEM)
    bf16, f32 = jnp.bfloat16, jnp.float32
    return pl.pallas_call(
        far_kernel,
        in_specs=[pl.BlockSpec(memory_space=pltpu.SMEM)]
        + [any_spec] * 6
        + [vmem_spec]
        + [any_spec] * 3
        + [vmem_spec],
        out_specs=[any_spec] * 8,
        out_shape=[jax.ShapeDtypeStruct((HALF, QUARTER), bf16)] * 8,
        scratch_shapes=[
            pltpu.VMEM((1, ROWS, QUARTER), bf16),
            pltpu.VMEM((QUARTER, HID), bf16),
            pltpu.VMEM((QUARTER, HID), bf16),
            pltpu.VMEM((4, HID, QUARTER), bf16),
            pltpu.VMEM((4, ROWS, QUARTER), bf16),
            pltpu.VMEM((ROWS, HID), f32),
            pltpu.VMEM((ROWS, HID), f32),
            pltpu.VMEM((ROWS, HID), bf16),
            pltpu.SemaphoreType.DMA((4,)),
            pltpu.SemaphoreType.DMA((6,)),
            pltpu.SemaphoreType.DMA((2,)),
            pltpu.SemaphoreType.DMA((4, 4)),
        ],
        compiler_params=pltpu.CompilerParams(vmem_limit_bytes=EXPERT_VMEM),
        cost_estimate=pl.CostEstimate(
            flops=0, bytes_accessed=0, transcendentals=0
        ),
        name="far",
    )(x_at, *pieces, *sums, wg, wu, wd, inv_gain)


def finish_kernel(h, back, ids_col, ids_row, out):
    slot_col = slots_of(ids_col[...], ids_row[...], 1)
    slot = lax.broadcasted_iota(jnp.int32, (TOK, SLOTS), 1)
    pick = jnp.where(slot == slot_col, 1.0, 0.0).astype(jnp.bfloat16)
    moe = mm(pick, back[...])
    out[...] = (h[...].astype(jnp.float32) + moe).astype(jnp.bfloat16)


def finish(h, back, ids):
    return pl.pallas_call(
        finish_kernel,
        grid=(QUARTER // LANES,),
        in_specs=[
            pl.BlockSpec((TOK, LANES), lambda i: (0, i)),
            pl.BlockSpec((SLOTS, LANES), lambda i: (0, i)),
            pl.BlockSpec((TOK, 1), lambda i: (0, 0)),
            pl.BlockSpec((1, TOK), lambda i: (0, 0)),
        ],
        out_specs=pl.BlockSpec((TOK, LANES), lambda i: (0, i)),
        out_shape=jax.ShapeDtypeStruct((TOK, QUARTER), jnp.bfloat16),
        compiler_params=pltpu.CompilerParams(vmem_limit_bytes=30 << 20),
        name="finish",
    )(h, back, ids.reshape(TOK, 1), ids.reshape(1, TOK))


def along_x(block, step):
    return lax.ppermute(block, "x", [(i, (i + step) % 4) for i in range(4)])


def other_core(block):
    return lax.ppermute(block, "c", [(0, 1), (1, 0)])


def add(*terms):
    total = terms[0].astype(jnp.float32)
    for term in terms[1:]:
        total = total + term.astype(jnp.float32)
    return total.astype(jnp.bfloat16)


def after(values, *earlier):
    return list(lax.optimization_barrier((tuple(values), earlier))[0])


def core_sums(outs):
    return [add(outs[j], other_core(outs[4 + j])) for j in range(4)]


def body(
    projected, short_filter, long_filter, residual_in, norm_gain, expert_ids,
    gate_weight, up_weight, down_weight,
):
    x_at = lax.axis_index("x").astype(jnp.int32).reshape(1)
    fwd, bck = (jnp.asarray(table) for table in dft_matrices())
    edge = jnp.concatenate(
        [projected[1, TOK - HALO :], projected[2, TOK - HALO :], projected[0, TOK - QHALO :]],
        axis=0,
    )
    halo = lax.ppermute(edge, ("z", "y", "c"), [(i, i + 1) for i in range(31)])
    spec, filt = spectrum(projected, short_filter, long_filter, fwd)
    h, send = front(
        x_at, projected, halo, short_filter, spec, filt, residual_in, norm_gain, expert_ids,
        fwd, bck,
    )
    got = lax.all_to_all(
        send.reshape(EXPERTS, CAP, QUARTER), ("z", "y"), split_axis=0, concat_axis=0, tiled=True
    ).reshape(SLOTS, QUARTER)
    inv_gain = (1.0 / norm_gain).reshape(4, 1, QUARTER)
    wg, wu, wd = gate_weight[0], up_weight[0], down_weight[0]

    def near_of(own, left, right):
        swapped = [other_core(p) for p in (own, left, right)]
        return near(x_at, [own, left, right, *swapped], wg, wu, inv_gain)

    def far_of(pieces, sums):
        swapped = [other_core(p) for p in pieces]
        return far(x_at, [*pieces, *swapped], sums, wg, wu, wd, inv_gain)

    def forward(left, right):
        return [along_x(left[:MID], 1), along_x(right[MID:], -1)]

    def second_wave(sums, to_right, to_left):
        lower = along_x(add(sums[2][:MID], to_right[:MID]), 1)
        upper = along_x(add(sums[2][MID:], to_left[MID:]), -1)
        return [
            add(sums[3][:MID], lower, to_left[:MID]),
            add(sums[3][MID:], to_right[MID:], upper),
        ]

    own0, own1 = got[:HALF], got[HALF:]
    left0, right0 = along_x(own0, 1), along_x(own0, -1)
    (own1,) = after([own1], left0, right0)
    far0 = forward(left0, right0)
    left1, right1 = along_x(own1, 1), along_x(own1, -1)
    part0 = near_of(own0, left0, right0)
    far0 = after(far0, part0[2])
    outs0 = far_of(far0, part0)
    own1, left1, right1 = after([own1, left1, right1], outs0[0])
    far1 = forward(left1, right1)
    sums0 = core_sums(outs0)
    own1, left1, right1 = after([own1, left1, right1], *sums0[:2])
    wave0 = [along_x(sums0[0], 1), along_x(sums0[1], -1)]
    part1 = near_of(own1, left1, right1)
    far1 = after(far1, part1[2])
    outs1 = far_of(far1, part1)
    wave0 = after(wave0, outs1[0])
    sums1 = core_sums(outs1)
    done0 = second_wave(sums0, *wave0)
    wave1 = [along_x(sums1[0], 1), along_x(sums1[1], -1)]
    done1 = second_wave(sums1, *wave1)
    back = lax.all_to_all(
        jnp.concatenate(done0 + done1, axis=0).reshape(EXPERTS, CAP, QUARTER),
        ("z", "y"), split_axis=0, concat_axis=0, tiled=True,
    ).reshape(SLOTS, QUARTER)
    return finish(h, back, expert_ids)


def solution(mesh):
    grid = Mesh(mesh.devices.reshape(4, 4, 2, 4), ("z", "y", "c", "x"))
    ctx = ("z", "y", "c")
    return jax.shard_map(
        body,
        mesh=grid,
        in_specs=(
            P(None, ctx, "x"),
            P(None, None, "x"),
            P(None, "x"),
            P(ctx, "x"),
            P(),
            P(ctx),
            P(ctx, None, "x"),
            P(ctx, None, "x"),
            P(ctx, "x", None),
        ),
        out_specs=P(ctx, "x"),
        check_vma=False,
    )
```

```python
import jax
import jax.numpy as jnp
import numpy as np
from jax import lax
from jax.experimental import pallas as pl
from jax.experimental.pallas import tpu as pltpu
from jax.sharding import Mesh
from jax.sharding import PartitionSpec as P

D = 4096
TAPS = 128
TOK = 256
QUARTER = 1024
HID = 768
EXPERTS = 16
CAP = 40
SLOTS = EXPERTS * CAP
SPAN = TOK + TAPS
BINS = 200
HALO = 144
QHALO = 16
LANES = 512
HALF = 320
ROWS = 2 * HALF


def dft_matrices():
    n = np.arange(SPAN)
    k = np.arange(BINS)
    angle = 2 * np.pi * ((k[:, None] * n[None, :]) % SPAN) / SPAN
    live = (k <= SPAN // 2)[:, None]
    forward = np.concatenate([np.cos(angle) * live, -np.sin(angle) * live], axis=0)
    weight = np.where((k == 0) | (k == SPAN // 2), 1.0, 2.0) * (k <= SPAN // 2) / SPAN
    back = np.concatenate(
        [np.cos(angle).T[TAPS:] * weight, -np.sin(angle).T[TAPS:] * weight], axis=1
    )
    return split_np(forward.astype(np.float32)), split_np(back.astype(np.float32))


def split_np(value):
    high = value.astype(jnp.bfloat16)
    low = (value - high.astype(np.float32)).astype(jnp.bfloat16)
    return np.stack([high, low])


def split(value):
    high = value.astype(jnp.bfloat16)
    return high, (value - high.astype(jnp.float32)).astype(jnp.bfloat16)


def mm(a, b):
    return jnp.dot(a, b, preferred_element_type=jnp.float32)


def mm_split(a, b):
    high, low = split(b)
    return mm(a[0], high) + (mm(a[0], low) + mm(a[1], high))


def slots_of(ids_col, ids_row, axis):
    first = lax.broadcasted_iota(jnp.int32, (TOK, TOK), 0)
    second = lax.broadcasted_iota(jnp.int32, (TOK, TOK), 1)
    same = ids_col == ids_row
    earlier = (first < second) if axis == 0 else (second < first)
    rank = jnp.sum(jnp.where(same & earlier, 1.0, 0.0), axis=axis, keepdims=True)
    ids = ids_row if axis == 0 else ids_col
    return ids * CAP + rank.astype(jnp.int32)


def taps3(ext, filt, start, length):
    return (
        filt[0:1] * ext[start : start + length]
        + filt[1:2] * ext[start - 1 : start - 1 + length]
        + filt[2:3] * ext[start - 2 : start - 2 + length]
    )


def spectrum_kernel(proj, short, long_f, fwd, spec_out, filt_out, table, sem):
    copy = pltpu.make_async_copy(fwd, table, sem)

    @pl.when(pl.program_id(0) == 0)
    def _():
        copy.start()

    zeros = jnp.zeros((8, LANES), jnp.float32)

    def filtered(f):
        ext = jnp.concatenate([zeros, proj[f].astype(jnp.float32)], axis=0)
        return taps3(ext, short[f], 8, TOK)

    live = lax.broadcasted_iota(jnp.int32, (TOK, LANES), 0) >= 2
    kv = jnp.where(live, filtered(1) * filtered(2), 0.0).astype(jnp.bfloat16)

    @pl.when(pl.program_id(0) == 0)
    def _():
        copy.wait()

    filt_out[...] = mm_split((table[0, :, :TAPS], table[1, :, :TAPS]), long_f[...])
    spec_out[...] = mm(table[0, :, TAPS:], kv) + mm(table[1, :, TAPS:], kv)


def spectrum(projected, short, long_f, fwd):
    steps = QUARTER // LANES
    return pl.pallas_call(
        spectrum_kernel,
        grid=(steps,),
        in_specs=[
            pl.BlockSpec((3, TOK, LANES), lambda i: (0, 0, i)),
            pl.BlockSpec((3, 3, LANES), lambda i: (0, 0, i)),
            pl.BlockSpec((TAPS, LANES), lambda i: (0, i)),
            pl.BlockSpec(memory_space=pltpu.HBM),
        ],
        out_specs=[pl.BlockSpec((2 * BINS, LANES), lambda i: (0, i))] * 2,
        out_shape=[jax.ShapeDtypeStruct((2 * BINS, QUARTER), jnp.float32)] * 2,
        scratch_shapes=[
            pltpu.VMEM((2, 2 * BINS, SPAN), jnp.bfloat16),
            pltpu.SemaphoreType.DMA,
        ],
        compiler_params=pltpu.CompilerParams(vmem_limit_bytes=60 << 20),
        cost_estimate=pl.CostEstimate(
            flops=4 << 30, bytes_accessed=8 << 20, transcendentals=0
        ),
        name="spectrum",
    )(projected, short, long_f, fwd)


def front_kernel(
    x_ref, proj, halo, short, spec, filt, res, gain, ids_col, ids_row,
    fwd, back, h_out, send_out, fwd_table, back_table, sems,
):
    f32 = jnp.float32
    copies = [
        pltpu.make_async_copy(fwd, fwd_table, sems.at[0]),
        pltpu.make_async_copy(back, back_table, sems.at[1]),
    ]

    @pl.when(pl.program_id(0) == 0)
    def _():
        for copy in copies:
            copy.start()

    def filtered(f):
        ext = jnp.concatenate([halo[(f - 1) * HALO : f * HALO], proj[f, :QHALO]], axis=0).astype(f32)
        return taps3(ext, short[f], HALO - TAPS, HALO)

    live = lax.broadcasted_iota(jnp.int32, (HALO, LANES), 0) < TAPS + 2
    kv = jnp.where(live, filtered(1) * filtered(2), 0.0).astype(jnp.bfloat16)
    ext = jnp.concatenate([halo[2 * HALO :], proj[0]], axis=0).astype(f32)
    s0 = taps3(ext, short[0], QHALO, TOK)

    @pl.when(pl.program_id(0) == 0)
    def _():
        for copy in copies:
            copy.wait()

    total = spec[...] + mm(fwd_table[0, :, :HALO], kv) + mm(fwd_table[1, :, :HALO], kv)
    re, im = total[:BINS], total[BINS:]
    fre, fim = filt[:BINS], filt[BINS:]
    prod = jnp.concatenate([re * fre - im * fim, re * fim + im * fre], axis=0)
    long_out = mm_split((back_table[0], back_table[1]), prod)
    h = (res[...].astype(f32) + s0 * long_out).astype(jnp.bfloat16)
    h_out[...] = h
    gained = (h.astype(f32) * gain[...]).astype(jnp.bfloat16)
    slot_row = slots_of(ids_col[...], ids_row[...], 0)
    slot = lax.broadcasted_iota(jnp.int32, (SLOTS, TOK), 0)
    pick = jnp.where(slot == slot_row, 1.0, 0.0).astype(jnp.bfloat16)
    send_out[...] = mm(pick, gained).astype(jnp.bfloat16)


def front(x_at, projected, halo, short, spec, filt, res, gain, ids, fwd, back):
    steps = QUARTER // LANES

    def whole(shape):
        return pl.BlockSpec(shape, lambda i, x: (0,) * len(shape))

    def columns(rows):
        return pl.BlockSpec((rows, LANES), lambda i, x: (0, i))

    return pl.pallas_call(
        front_kernel,
        grid_spec=pltpu.PrefetchScalarGridSpec(
            num_scalar_prefetch=1,
            grid=(steps,),
            in_specs=[
                pl.BlockSpec((3, TOK, LANES), lambda i, x: (0, 0, i)),
                columns(2 * HALO + QHALO),
                pl.BlockSpec((3, 3, LANES), lambda i, x: (0, 0, i)),
                columns(2 * BINS),
                columns(2 * BINS),
                columns(TOK),
                pl.BlockSpec((1, LANES), lambda i, x: (0, x[0] * steps + i)),
                whole((TOK, 1)),
                whole((1, TOK)),
                pl.BlockSpec(memory_space=pltpu.HBM),
                pl.BlockSpec(memory_space=pltpu.HBM),
            ],
            out_specs=[columns(TOK), columns(SLOTS)],
            scratch_shapes=[
                pltpu.VMEM((2, 2 * BINS, SPAN), jnp.bfloat16),
                pltpu.VMEM((2, TOK, 2 * BINS), jnp.bfloat16),
                pltpu.SemaphoreType.DMA((2,)),
            ],
        ),
        out_shape=[
            jax.ShapeDtypeStruct((TOK, QUARTER), jnp.bfloat16),
            jax.ShapeDtypeStruct((SLOTS, QUARTER), jnp.bfloat16),
        ],
        compiler_params=pltpu.CompilerParams(vmem_limit_bytes=60 << 20),
        name="front",
    )(
        x_at, projected, halo, short, spec, filt, res, gain.reshape(1, D),
        ids.reshape(TOK, 1), ids.reshape(1, TOK), fwd, back,
    )


MID = HALF // 2
K_OFFSET = (0, 3, 1, 2)
N_OFFSET = (2, 1, 3, 0)
EXPERT_VMEM = 42 << 20
LAYOUT = ((0, 0, HALF), (1, 0, HALF), (2, 0, HALF), (3, 0, MID), (3, MID, MID))


def aligned(q):
    return pl.ds(pl.multiple_of(q * QUARTER, QUARTER), QUARTER)


def add_squares(squares, xk, ig):
    h = xk.astype(jnp.float32) * ig
    sq = h * h
    for c in range(QUARTER // 128):
        squares = squares + sq[:, c * 128 : (c + 1) * 128]
    return squares


def expert_kernel(x_ref, *refs):
    count = 2 * len(LAYOUT)
    pieces = refs[:count]
    wg, wu, wd, ig = refs[count : count + 4]
    outs = refs[count + 4 : count + 12]
    xs, wgs, wus, wds, ys, accg, accu, hid, x_sem, w_sem, y_sem = refs[count + 12 :]

    k_at = [lax.rem(x_ref[0] + off, 4) for off in K_OFFSET]
    n_at = [lax.rem(x_ref[0] + off, 4) for off in N_OFFSET]
    x_copies = [[] for _ in range(4)]
    for core in range(2):
        for n, (block, start, rows) in enumerate(LAYOUT):
            at = core * len(LAYOUT) + n
            x_copies[block].append(
                pltpu.make_async_copy(
                    pieces[at], xs.at[block, pl.ds(core * HALF + start, rows)], x_sem.at[at]
                )
            )
    w_copies = [
        [
            pltpu.make_async_copy(wg.at[aligned(k_at[k])], wgs.at[k], w_sem.at[0, k]),
            pltpu.make_async_copy(wu.at[aligned(k_at[k])], wus.at[k], w_sem.at[1, k]),
        ]
        for k in range(4)
    ]
    d_copies = [
        pltpu.make_async_copy(wd.at[:, aligned(n_at[j])], wds.at[j], w_sem.at[2, j])
        for j in range(4)
    ]
    places = {
        (0, 0): (0, 0), (0, 1): (1, 1), (1, 0): (2, 0), (1, 1): (0, 1),
        (2, 0): (1, 0), (2, 1): (2, 1), (3, 0): (3, 0), (3, 1): (3, 1),
    }
    y_copies = [[] for _ in range(4)]
    for (j, upper), (out, at) in places.items():
        for core in range(2):
            y_copies[j].append(
                pltpu.make_async_copy(
                    ys.at[j, pl.ds(core * HALF + upper * MID, MID)],
                    outs[core * 4 + out].at[pl.ds(at * MID, MID)],
                    y_sem.at[j, core * 2 + upper],
                )
            )
    for k in range(4):
        for copy in x_copies[k] + w_copies[k]:
            copy.start()
    for copy in d_copies:
        copy.start()

    squares = jnp.zeros((ROWS, 128), jnp.float32)
    for k in range(4):
        for copy in x_copies[k] + w_copies[k]:
            copy.wait()
        xk = xs[k]
        g = mm(xk, wgs[k])
        u = mm(xk, wus[k])
        squares = add_squares(squares, xk, ig[k_at[k]])
        if k == 0:
            accg[...] = g
            accu[...] = u
        elif k < 3:
            accg[...] += g
            accu[...] += u
        else:
            scale = lax.rsqrt(jnp.sum(squares, axis=1, keepdims=True) / D + 1e-06)
            gate = (accg[...] + g) * scale
            up = (accu[...] + u) * scale
            hid[...] = (gate / (1.0 + jnp.exp(-gate)) * up).astype(jnp.bfloat16)
    for j in range(4):
        d_copies[j].wait()
        ys[j] = mm(hid[...], wds[j]).astype(jnp.bfloat16)
        for copy in y_copies[j]:
            copy.start()
    for j in range(4):
        for copy in y_copies[j]:
            copy.wait()


def expert(x_at, pieces, wg, wu, wd, inv_gain):
    any_spec = pl.BlockSpec(memory_space=pl.ANY)
    bf16 = jnp.bfloat16
    return pl.pallas_call(
        expert_kernel,
        in_specs=[pl.BlockSpec(memory_space=pltpu.SMEM)]
        + [any_spec] * (len(pieces) + 3)
        + [pl.BlockSpec(memory_space=pltpu.VMEM)],
        out_specs=[any_spec] * 8,
        out_shape=[jax.ShapeDtypeStruct((HALF, QUARTER), bf16)] * 8,
        scratch_shapes=[
            pltpu.VMEM((4, ROWS, QUARTER), bf16),
            pltpu.VMEM((4, QUARTER, HID), bf16),
            pltpu.VMEM((4, QUARTER, HID), bf16),
            pltpu.VMEM((4, HID, QUARTER), bf16),
            pltpu.VMEM((4, ROWS, QUARTER), bf16),
            pltpu.VMEM((ROWS, HID), jnp.float32),
            pltpu.VMEM((ROWS, HID), jnp.float32),
            pltpu.VMEM((ROWS, HID), bf16),
            pltpu.SemaphoreType.DMA((len(pieces),)),
            pltpu.SemaphoreType.DMA((3, 4)),
            pltpu.SemaphoreType.DMA((4, 4)),
        ],
        compiler_params=pltpu.CompilerParams(vmem_limit_bytes=EXPERT_VMEM),
        cost_estimate=pl.CostEstimate(flops=0, bytes_accessed=0, transcendentals=0),
        name="expert",
    )(x_at, *pieces, wg, wu, wd, inv_gain)


def finish_kernel(h, back, ids_col, ids_row, out):
    slot_col = slots_of(ids_col[...], ids_row[...], 1)
    slot = lax.broadcasted_iota(jnp.int32, (TOK, SLOTS), 1)
    pick = jnp.where(slot == slot_col, 1.0, 0.0).astype(jnp.bfloat16)
    moe = mm(pick, back[...])
    out[...] = (h[...].astype(jnp.float32) + moe).astype(jnp.bfloat16)


def finish(h, back, ids):
    return pl.pallas_call(
        finish_kernel,
        grid=(QUARTER // LANES,),
        in_specs=[
            pl.BlockSpec((TOK, LANES), lambda i: (0, i)),
            pl.BlockSpec((SLOTS, LANES), lambda i: (0, i)),
            pl.BlockSpec((TOK, 1), lambda i: (0, 0)),
            pl.BlockSpec((1, TOK), lambda i: (0, 0)),
        ],
        out_specs=pl.BlockSpec((TOK, LANES), lambda i: (0, i)),
        out_shape=jax.ShapeDtypeStruct((TOK, QUARTER), jnp.bfloat16),
        compiler_params=pltpu.CompilerParams(vmem_limit_bytes=30 << 20),
        name="finish",
    )(h, back, ids.reshape(TOK, 1), ids.reshape(1, TOK))


def along_x(block, step):
    return lax.ppermute(block, "x", [(i, (i + step) % 4) for i in range(4)])


def other_core(block):
    return lax.ppermute(block, "c", [(0, 1), (1, 0)])


def add(*terms):
    total = terms[0].astype(jnp.float32)
    for term in terms[1:]:
        total = total + term.astype(jnp.float32)
    return total.astype(jnp.bfloat16)


def after(values, *earlier):
    return list(lax.optimization_barrier((tuple(values), earlier))[0])


def core_sums(outs):
    return [add(outs[j], other_core(outs[4 + j])) for j in range(4)]


def body(
    projected, short_filter, long_filter, residual_in, norm_gain, expert_ids,
    gate_weight, up_weight, down_weight,
):
    x_at = lax.axis_index("x").astype(jnp.int32).reshape(1)
    fwd, bck = (jnp.asarray(table) for table in dft_matrices())
    edge = jnp.concatenate(
        [projected[1, TOK - HALO :], projected[2, TOK - HALO :], projected[0, TOK - QHALO :]],
        axis=0,
    )
    halo = lax.ppermute(edge, ("z", "y", "c"), [(i, i + 1) for i in range(31)])
    spec, filt = spectrum(projected, short_filter, long_filter, fwd)
    h, send = front(
        x_at, projected, halo, short_filter, spec, filt, residual_in, norm_gain, expert_ids,
        fwd, bck,
    )
    got = lax.all_to_all(
        send.reshape(EXPERTS, CAP, QUARTER), ("z", "y"), split_axis=0, concat_axis=0, tiled=True
    ).reshape(SLOTS, QUARTER)
    inv_gain = (1.0 / norm_gain).reshape(4, 1, QUARTER)
    wg, wu, wd = gate_weight[0], up_weight[0], down_weight[0]

    def both_cores(pieces):
        return [*pieces, *(other_core(p) for p in pieces)]

    def expert_of(pieces):
        return expert(x_at, pieces, wg, wu, wd, inv_gain)

    def forward(left, right):
        return [along_x(left[:MID], 1), along_x(right[MID:], -1)]

    def second_wave(sums, to_right, to_left):
        lower = along_x(add(sums[2][:MID], to_right[:MID]), 1)
        upper = along_x(add(sums[2][MID:], to_left[MID:]), -1)
        return [
            add(sums[3][:MID], lower, to_left[:MID]),
            add(sums[3][MID:], to_right[MID:], upper),
        ]

    own0, own1 = got[:HALF], got[HALF:]
    left0, right0 = along_x(own0, 1), along_x(own0, -1)
    (own1,) = after([own1], left0, right0)
    far0 = forward(left0, right0)
    left1, right1 = along_x(own1, 1), along_x(own1, -1)
    outs0 = expert_of(both_cores([own0, left0, right0, *far0]))
    own1, left1, right1 = after([own1, left1, right1], outs0[0])
    far1 = forward(left1, right1)
    sums0 = core_sums(outs0)
    pieces1 = after(both_cores([own1, left1, right1, *far1]), *sums0[:2])
    wave0 = [along_x(sums0[0], 1), along_x(sums0[1], -1)]
    outs1 = expert_of(pieces1)
    wave0 = after(wave0, outs1[0])
    sums1 = core_sums(outs1)
    done0 = second_wave(sums0, *wave0)
    wave1 = [along_x(sums1[0], 1), along_x(sums1[1], -1)]
    done1 = second_wave(sums1, *wave1)
    back = lax.all_to_all(
        jnp.concatenate(done0 + done1, axis=0).reshape(EXPERTS, CAP, QUARTER),
        ("z", "y"), split_axis=0, concat_axis=0, tiled=True,
    ).reshape(SLOTS, QUARTER)
    return finish(h, back, expert_ids)


def solution(mesh):
    grid = Mesh(mesh.devices.reshape(4, 4, 2, 4), ("z", "y", "c", "x"))
    ctx = ("z", "y", "c")
    return jax.shard_map(
        body,
        mesh=grid,
        in_specs=(
            P(None, ctx, "x"),
            P(None, None, "x"),
            P(None, "x"),
            P(ctx, "x"),
            P(),
            P(ctx),
            P(ctx, None, "x"),
            P(ctx, None, "x"),
            P(ctx, "x", None),
        ),
        out_specs=P(ctx, "x"),
        check_vma=False,
    )
```

```python
import functools

import jax
import jax.numpy as jnp
import numpy as np
from jax import lax
from jax.experimental import pallas as pl
from jax.experimental.pallas import tpu as pltpu
from jax.sharding import Mesh
from jax.sharding import PartitionSpec as P

D = 4096
TAPS = 128
TOK = 256
QUARTER = 1024
HID = 768
EXPERTS = 16
CAP = 40
SLOTS = EXPERTS * CAP
SPAN = TOK + TAPS
BINS = 200
HALO = 144
QHALO = 16
LANES = 512
SPLIT = 320


def dft_matrices():
    n = np.arange(SPAN)
    k = np.arange(BINS)
    angle = 2 * np.pi * ((k[:, None] * n[None, :]) % SPAN) / SPAN
    live = (k <= SPAN // 2)[:, None]
    forward = np.concatenate([np.cos(angle) * live, -np.sin(angle) * live], axis=0)
    weight = np.where((k == 0) | (k == SPAN // 2), 1.0, 2.0) * (k <= SPAN // 2) / SPAN
    back = np.concatenate(
        [np.cos(angle).T[TAPS:] * weight, -np.sin(angle).T[TAPS:] * weight], axis=1
    )
    return split_np(forward.astype(np.float32)), split_np(back.astype(np.float32))


def split_np(value):
    high = value.astype(jnp.bfloat16)
    low = (value - high.astype(np.float32)).astype(jnp.bfloat16)
    return np.stack([high, low])


def split(value):
    high = value.astype(jnp.bfloat16)
    return high, (value - high.astype(jnp.float32)).astype(jnp.bfloat16)


def mm(a, b):
    return jnp.dot(a, b, preferred_element_type=jnp.float32)


def mm_split(a, b):
    high, low = split(b)
    return mm(a[0], high) + (mm(a[0], low) + mm(a[1], high))


def slots_of(ids_col, ids_row, axis):
    first = lax.broadcasted_iota(jnp.int32, (TOK, TOK), 0)
    second = lax.broadcasted_iota(jnp.int32, (TOK, TOK), 1)
    same = ids_col == ids_row
    earlier = (first < second) if axis == 0 else (second < first)
    rank = jnp.sum(jnp.where(same & earlier, 1.0, 0.0), axis=axis, keepdims=True)
    ids = ids_row if axis == 0 else ids_col
    return ids * CAP + rank.astype(jnp.int32)


def taps3(ext, filt, start, length):
    return (
        filt[0:1] * ext[start : start + length]
        + filt[1:2] * ext[start - 1 : start - 1 + length]
        + filt[2:3] * ext[start - 2 : start - 2 + length]
    )


def spectrum_kernel(proj, short, long_f, fwd, spec_out, filt_out, table, sem):
    copy = pltpu.make_async_copy(fwd, table, sem)

    @pl.when(pl.program_id(0) == 0)
    def _():
        copy.start()

    zeros = jnp.zeros((8, LANES), jnp.float32)

    def filtered(f):
        ext = jnp.concatenate([zeros, proj[f].astype(jnp.float32)], axis=0)
        return taps3(ext, short[f], 8, TOK)

    live = lax.broadcasted_iota(jnp.int32, (TOK, LANES), 0) >= 2
    kv = jnp.where(live, filtered(1) * filtered(2), 0.0).astype(jnp.bfloat16)

    @pl.when(pl.program_id(0) == 0)
    def _():
        copy.wait()

    filt_out[...] = mm_split((table[0, :, :TAPS], table[1, :, :TAPS]), long_f[...])
    spec_out[...] = mm(table[0, :, TAPS:], kv) + mm(table[1, :, TAPS:], kv)


def spectrum(projected, short, long_f, fwd):
    steps = QUARTER // LANES
    return pl.pallas_call(
        spectrum_kernel,
        grid=(steps,),
        in_specs=[
            pl.BlockSpec((3, TOK, LANES), lambda i: (0, 0, i)),
            pl.BlockSpec((3, 3, LANES), lambda i: (0, 0, i)),
            pl.BlockSpec((TAPS, LANES), lambda i: (0, i)),
            pl.BlockSpec(memory_space=pltpu.HBM),
        ],
        out_specs=[pl.BlockSpec((2 * BINS, LANES), lambda i: (0, i))] * 2,
        out_shape=[jax.ShapeDtypeStruct((2 * BINS, QUARTER), jnp.float32)] * 2,
        scratch_shapes=[
            pltpu.VMEM((2, 2 * BINS, SPAN), jnp.bfloat16),
            pltpu.SemaphoreType.DMA,
        ],
        compiler_params=pltpu.CompilerParams(vmem_limit_bytes=60 << 20),
        cost_estimate=pl.CostEstimate(
            flops=4 << 30, bytes_accessed=8 << 20, transcendentals=0
        ),
        name="spectrum",
    )(projected, short, long_f, fwd)


def front_kernel(
    x_ref, proj, halo, short, spec, filt, res, gain, ids_col, ids_row,
    fwd, back, h_out, send_out, fwd_table, back_table, sems,
):
    f32 = jnp.float32
    copies = [
        pltpu.make_async_copy(fwd, fwd_table, sems.at[0]),
        pltpu.make_async_copy(back, back_table, sems.at[1]),
    ]

    @pl.when(pl.program_id(0) == 0)
    def _():
        for copy in copies:
            copy.start()

    def filtered(f):
        ext = jnp.concatenate([halo[(f - 1) * HALO : f * HALO], proj[f, :QHALO]], axis=0).astype(f32)
        return taps3(ext, short[f], HALO - TAPS, HALO)

    live = lax.broadcasted_iota(jnp.int32, (HALO, LANES), 0) < TAPS + 2
    kv = jnp.where(live, filtered(1) * filtered(2), 0.0).astype(jnp.bfloat16)
    ext = jnp.concatenate([halo[2 * HALO :], proj[0]], axis=0).astype(f32)
    s0 = taps3(ext, short[0], QHALO, TOK)

    @pl.when(pl.program_id(0) == 0)
    def _():
        for copy in copies:
            copy.wait()

    total = spec[...] + mm(fwd_table[0, :, :HALO], kv) + mm(fwd_table[1, :, :HALO], kv)
    re, im = total[:BINS], total[BINS:]
    fre, fim = filt[:BINS], filt[BINS:]
    prod = jnp.concatenate([re * fre - im * fim, re * fim + im * fre], axis=0)
    long_out = mm_split((back_table[0], back_table[1]), prod)
    h = (res[...].astype(f32) + s0 * long_out).astype(jnp.bfloat16)
    h_out[...] = h
    gained = (h.astype(f32) * gain[...]).astype(jnp.bfloat16)
    slot_row = slots_of(ids_col[...], ids_row[...], 0)
    slot = lax.broadcasted_iota(jnp.int32, (SLOTS, TOK), 0)
    pick = jnp.where(slot == slot_row, 1.0, 0.0).astype(jnp.bfloat16)
    send_out[...] = mm(pick, gained).astype(jnp.bfloat16)


def front(x_at, projected, halo, short, spec, filt, res, gain, ids, fwd, back):
    steps = QUARTER // LANES

    def whole(shape):
        return pl.BlockSpec(shape, lambda i, x: (0,) * len(shape))

    def columns(rows):
        return pl.BlockSpec((rows, LANES), lambda i, x: (0, i))

    return pl.pallas_call(
        front_kernel,
        grid_spec=pltpu.PrefetchScalarGridSpec(
            num_scalar_prefetch=1,
            grid=(steps,),
            in_specs=[
                pl.BlockSpec((3, TOK, LANES), lambda i, x: (0, 0, i)),
                columns(2 * HALO + QHALO),
                pl.BlockSpec((3, 3, LANES), lambda i, x: (0, 0, i)),
                columns(2 * BINS),
                columns(2 * BINS),
                columns(TOK),
                pl.BlockSpec((1, LANES), lambda i, x: (0, x[0] * steps + i)),
                whole((TOK, 1)),
                whole((1, TOK)),
                pl.BlockSpec(memory_space=pltpu.HBM),
                pl.BlockSpec(memory_space=pltpu.HBM),
            ],
            out_specs=[columns(TOK), columns(SLOTS)],
            scratch_shapes=[
                pltpu.VMEM((2, 2 * BINS, SPAN), jnp.bfloat16),
                pltpu.VMEM((2, TOK, 2 * BINS), jnp.bfloat16),
                pltpu.SemaphoreType.DMA((2,)),
            ],
        ),
        out_shape=[
            jax.ShapeDtypeStruct((TOK, QUARTER), jnp.bfloat16),
            jax.ShapeDtypeStruct((SLOTS, QUARTER), jnp.bfloat16),
        ],
        compiler_params=pltpu.CompilerParams(vmem_limit_bytes=60 << 20),
        name="front",
    )(
        x_at, projected, halo, short, spec, filt, res, gain.reshape(1, D),
        ids.reshape(TOK, 1), ids.reshape(1, TOK), fwd, back,
    )


K_OFFSET = (0, 3, 1, 2)
N_OFFSET = (2, 1, 3, 0)
EXPERT_VMEM = 42 << 20


def middle(rows):
    return (rows // 2 + 15) // 16 * 16


def aligned(q):
    return pl.ds(pl.multiple_of(q * QUARTER, QUARTER), QUARTER)


def x_copy(piece, xs, block, start, sem):
    return pltpu.make_async_copy(piece, xs.at[block, pl.ds(start, piece.shape[0])], sem)


def add_squares(squares, xk, ig):
    h = xk.astype(jnp.float32) * ig
    sq = h * h
    for c in range(QUARTER // 128):
        squares = squares + sq[:, c * 128 : (c + 1) * 128]
    return squares


def near_kernel(x_ref, *refs):
    pieces = refs[:6]
    wg, wu, ig, g_out, u_out, sq_out, xs, wgs, wus, accg, accu, x_sem, w_sem, y_sem = refs[6:]
    rows = accg.shape[0]
    half = rows // 2
    k_at = [lax.rem(x_ref[0] + K_OFFSET[k], 4) for k in range(3)]
    copies = []
    for k in range(3):
        copies.append(
            [
                x_copy(pieces[k], xs, k, 0, x_sem.at[k]),
                x_copy(pieces[3 + k], xs, k, half, x_sem.at[3 + k]),
                pltpu.make_async_copy(wg.at[aligned(k_at[k])], wgs.at[k], w_sem.at[0, k]),
                pltpu.make_async_copy(wu.at[aligned(k_at[k])], wus.at[k], w_sem.at[1, k]),
            ]
        )
        for copy in copies[k]:
            copy.start()
    squares = jnp.zeros((rows, 128), jnp.float32)
    for k in range(3):
        for copy in copies[k]:
            copy.wait()
        g = mm(xs[k], wgs[k])
        u = mm(xs[k], wus[k])
        squares = add_squares(squares, xs[k], ig[k_at[k]])
        if k == 0:
            accg[...] = g
            accu[...] = u
        else:
            accg[...] += g
            accu[...] += u
    sq_out[...] = squares
    outs = [
        pltpu.make_async_copy(accg, g_out, y_sem.at[0]),
        pltpu.make_async_copy(accu, u_out, y_sem.at[1]),
    ]
    for copy in outs:
        copy.start()
    for copy in outs:
        copy.wait()


def near(x_at, pieces, wg, wu, inv_gain):
    rows = 2 * pieces[0].shape[0]
    any_spec = pl.BlockSpec(memory_space=pl.ANY)
    vmem_spec = pl.BlockSpec(memory_space=pltpu.VMEM)
    bf16, f32 = jnp.bfloat16, jnp.float32
    return pl.pallas_call(
        near_kernel,
        in_specs=[pl.BlockSpec(memory_space=pltpu.SMEM)] + [any_spec] * 8 + [vmem_spec],
        out_specs=[any_spec, any_spec, vmem_spec],
        out_shape=[
            jax.ShapeDtypeStruct((rows, HID), f32),
            jax.ShapeDtypeStruct((rows, HID), f32),
            jax.ShapeDtypeStruct((rows, 128), f32),
        ],
        scratch_shapes=[
            pltpu.VMEM((3, rows, QUARTER), bf16),
            pltpu.VMEM((3, QUARTER, HID), bf16),
            pltpu.VMEM((3, QUARTER, HID), bf16),
            pltpu.VMEM((rows, HID), f32),
            pltpu.VMEM((rows, HID), f32),
            pltpu.SemaphoreType.DMA((6,)),
            pltpu.SemaphoreType.DMA((2, 3)),
            pltpu.SemaphoreType.DMA((2,)),
        ],
        compiler_params=pltpu.CompilerParams(vmem_limit_bytes=EXPERT_VMEM),
        cost_estimate=pl.CostEstimate(
            flops=0, bytes_accessed=0, transcendentals=0
        ),
        name="near",
    )(x_at, *pieces, wg, wu, inv_gain)


def far_kernel(x_ref, *refs):
    pieces = refs[:4]
    g_in, u_in, sq_in, wg, wu, wd, ig = refs[4:11]
    outs = refs[11:19]
    xs, wgs, wus, wds, ys, accg, accu, hid, x_sem, w_sem, a_sem, y_sem = refs[19:]
    rows = accg.shape[0]
    half = rows // 2
    mid = middle(half)
    spans = (mid, half - mid)
    k_at = lax.rem(x_ref[0] + K_OFFSET[3], 4)
    first = [
        x_copy(pieces[n], xs, 0, n // 2 * half + n % 2 * mid, x_sem.at[n]) for n in range(4)
    ] + [
        pltpu.make_async_copy(wg.at[aligned(k_at)], wgs, w_sem.at[0]),
        pltpu.make_async_copy(wu.at[aligned(k_at)], wus, w_sem.at[1]),
    ]
    sums = [
        pltpu.make_async_copy(g_in, accg, a_sem.at[0]),
        pltpu.make_async_copy(u_in, accu, a_sem.at[1]),
    ]
    down = [
        pltpu.make_async_copy(
            wd.at[:, aligned(lax.rem(x_ref[0] + N_OFFSET[j], 4))], wds.at[j], w_sem.at[2 + j]
        )
        for j in range(4)
    ]
    for copy in first + sums + down:
        copy.start()

    places = {
        (0, 0): (0, 0), (0, 1): (1, 1), (1, 0): (2, 0), (1, 1): (0, 1),
        (2, 0): (1, 0), (2, 1): (2, 1), (3, 0): (3, 0), (3, 1): (3, 1),
    }
    results = [[] for _ in range(4)]
    for (j, upper), (out, at) in places.items():
        for core in range(2):
            results[j].append(
                pltpu.make_async_copy(
                    ys.at[j, pl.ds(core * half + upper * mid, spans[upper])],
                    outs[core * 4 + out].at[pl.ds(at * mid, spans[upper])],
                    y_sem.at[j, core * 2 + upper],
                )
            )
    for copy in first:
        copy.wait()
    xk = xs[0]
    g = mm(xk, wgs[...])
    u = mm(xk, wus[...])
    squares = add_squares(sq_in[...], xk, ig[k_at])
    scale = lax.rsqrt(jnp.sum(squares, axis=1, keepdims=True) / D + 1e-06)
    for copy in sums:
        copy.wait()
    gate = (accg[...] + g) * scale
    up = (accu[...] + u) * scale
    hid[...] = (gate / (1.0 + jnp.exp(-gate)) * up).astype(jnp.bfloat16)
    for j in range(4):
        down[j].wait()
        ys[j] = mm(hid[...], wds[j]).astype(jnp.bfloat16)
        for copy in results[j]:
            copy.start()
    for j in range(4):
        for copy in results[j]:
            copy.wait()


def far(x_at, pieces, sums, wg, wu, wd, inv_gain):
    rows = sums[0].shape[0]
    any_spec = pl.BlockSpec(memory_space=pl.ANY)
    vmem_spec = pl.BlockSpec(memory_space=pltpu.VMEM)
    bf16, f32 = jnp.bfloat16, jnp.float32
    return pl.pallas_call(
        far_kernel,
        in_specs=[pl.BlockSpec(memory_space=pltpu.SMEM)]
        + [any_spec] * 6
        + [vmem_spec]
        + [any_spec] * 3
        + [vmem_spec],
        out_specs=[any_spec] * 8,
        out_shape=[jax.ShapeDtypeStruct((rows // 2, QUARTER), bf16)] * 8,
        scratch_shapes=[
            pltpu.VMEM((1, rows, QUARTER), bf16),
            pltpu.VMEM((QUARTER, HID), bf16),
            pltpu.VMEM((QUARTER, HID), bf16),
            pltpu.VMEM((4, HID, QUARTER), bf16),
            pltpu.VMEM((4, rows, QUARTER), bf16),
            pltpu.VMEM((rows, HID), f32),
            pltpu.VMEM((rows, HID), f32),
            pltpu.VMEM((rows, HID), bf16),
            pltpu.SemaphoreType.DMA((4,)),
            pltpu.SemaphoreType.DMA((6,)),
            pltpu.SemaphoreType.DMA((2,)),
            pltpu.SemaphoreType.DMA((4, 4)),
        ],
        compiler_params=pltpu.CompilerParams(vmem_limit_bytes=EXPERT_VMEM),
        cost_estimate=pl.CostEstimate(
            flops=0, bytes_accessed=0, transcendentals=0
        ),
        name="far",
    )(x_at, *pieces, *sums, wg, wu, wd, inv_gain)


def finish_kernel(h, back, ids_col, ids_row, out):
    slot_col = slots_of(ids_col[...], ids_row[...], 1)
    slot = lax.broadcasted_iota(jnp.int32, (TOK, SLOTS), 1)
    pick = jnp.where(slot == slot_col, 1.0, 0.0).astype(jnp.bfloat16)
    moe = mm(pick, back[...])
    out[...] = (h[...].astype(jnp.float32) + moe).astype(jnp.bfloat16)


def finish(h, back, ids):
    return pl.pallas_call(
        finish_kernel,
        grid=(QUARTER // LANES,),
        in_specs=[
            pl.BlockSpec((TOK, LANES), lambda i: (0, i)),
            pl.BlockSpec((SLOTS, LANES), lambda i: (0, i)),
            pl.BlockSpec((TOK, 1), lambda i: (0, 0)),
            pl.BlockSpec((1, TOK), lambda i: (0, 0)),
        ],
        out_specs=pl.BlockSpec((TOK, LANES), lambda i: (0, i)),
        out_shape=jax.ShapeDtypeStruct((TOK, QUARTER), jnp.bfloat16),
        compiler_params=pltpu.CompilerParams(vmem_limit_bytes=30 << 20),
        name="finish",
    )(h, back, ids.reshape(TOK, 1), ids.reshape(1, TOK))


def along_x(block, step):
    return lax.ppermute(block, "x", [(i, (i + step) % 4) for i in range(4)])


def other_core(block):
    return lax.ppermute(block, "c", [(0, 1), (1, 0)])


def add(*terms):
    total = terms[0].astype(jnp.float32)
    for term in terms[1:]:
        total = total + term.astype(jnp.float32)
    return total.astype(jnp.bfloat16)


def after(values, *earlier):
    return list(lax.optimization_barrier((tuple(values), earlier))[0])


def core_sums(outs):
    return [add(outs[j], other_core(outs[4 + j])) for j in range(4)]


def body(
    projected, short_filter, long_filter, residual_in, norm_gain, expert_ids,
    gate_weight, up_weight, down_weight,
):
    x_at = lax.axis_index("x").astype(jnp.int32).reshape(1)
    fwd, bck = (jnp.asarray(table) for table in dft_matrices())
    edge = jnp.concatenate(
        [projected[1, TOK - HALO :], projected[2, TOK - HALO :], projected[0, TOK - QHALO :]],
        axis=0,
    )
    halo = lax.ppermute(edge, ("z", "y", "c"), [(i, i + 1) for i in range(31)])
    spec, filt = spectrum(projected, short_filter, long_filter, fwd)
    h, send = front(
        x_at, projected, halo, short_filter, spec, filt, residual_in, norm_gain, expert_ids,
        fwd, bck,
    )
    got = lax.all_to_all(
        send.reshape(EXPERTS, CAP, QUARTER), ("z", "y"), split_axis=0, concat_axis=0, tiled=True
    ).reshape(SLOTS, QUARTER)
    inv_gain = (1.0 / norm_gain).reshape(4, 1, QUARTER)
    wg, wu, wd = gate_weight[0], up_weight[0], down_weight[0]

    def both_cores(pieces):
        return [*pieces, *(other_core(p) for p in pieces)]

    def forward(left, right):
        mid = middle(left.shape[0])
        return [along_x(left[:mid], 1), along_x(right[mid:], -1)]

    def second_wave(sums, to_right, to_left):
        mid = middle(to_right.shape[0])
        lower = along_x(add(sums[2][:mid], to_right[:mid]), 1)
        upper = along_x(add(sums[2][mid:], to_left[mid:]), -1)
        return [
            add(sums[3][:mid], lower, to_left[:mid]),
            add(sums[3][mid:], to_right[mid:], upper),
        ]

    own0, own1 = got[:SPLIT], got[SPLIT:]
    left0, right0 = along_x(own0, 1), along_x(own0, -1)
    (own1,) = after([own1], left0, right0)
    far0 = forward(left0, right0)
    left1, right1 = along_x(own1, 1), along_x(own1, -1)
    part0 = near(x_at, both_cores([own0, left0, right0]), wg, wu, inv_gain)
    far0 = after(far0, part0[2])
    outs0 = far(x_at, both_cores(far0), part0, wg, wu, wd, inv_gain)
    twin1 = other_core(own1)
    left1, right1 = after([left1, right1], outs0[0])
    far1 = forward(left1, right1)
    sums0 = core_sums(outs0)
    part1 = near(x_at, [own1, left1, right1, twin1, other_core(left1), other_core(right1)], wg, wu, inv_gain)
    far1 = after(far1, part1[2], *sums0[:2])
    wave0 = [along_x(sums0[0], 1), along_x(sums0[1], -1)]
    outs1 = far(x_at, both_cores(far1), part1, wg, wu, wd, inv_gain)
    wave0 = after(wave0, outs1[0])
    sums1 = core_sums(outs1)
    done0 = second_wave(sums0, *wave0)
    wave1 = [along_x(sums1[0], 1), along_x(sums1[1], -1)]
    done1 = second_wave(sums1, *wave1)
    back = lax.all_to_all(
        jnp.concatenate(done0 + done1, axis=0).reshape(EXPERTS, CAP, QUARTER),
        ("z", "y"), split_axis=0, concat_axis=0, tiled=True,
    ).reshape(SLOTS, QUARTER)
    return finish(h, back, expert_ids)


def solution(mesh):
    grid = Mesh(mesh.devices.reshape(4, 4, 2, 4), ("z", "y", "c", "x"))
    ctx = ("z", "y", "c")
    return jax.shard_map(
        body,
        mesh=grid,
        in_specs=(
            P(None, ctx, "x"),
            P(None, None, "x"),
            P(None, "x"),
            P(ctx, "x"),
            P(),
            P(ctx),
            P(ctx, None, "x"),
            P(ctx, None, "x"),
            P(ctx, "x", None),
        ),
        out_specs=P(ctx, "x"),
        check_vma=False,
    )
```

```python
import functools

import jax
import jax.numpy as jnp
import numpy as np
from jax import lax
from jax.experimental import pallas as pl
from jax.experimental.pallas import tpu as pltpu
from jax.sharding import Mesh
from jax.sharding import PartitionSpec as P

D = 4096
TAPS = 128
TOK = 256
QUARTER = 1024
HID = 768
EXPERTS = 16
CAP = 40
SLOTS = EXPERTS * CAP
SPAN = TOK + TAPS
BINS = 200
HALO = 144
QHALO = 16
LANES = 512
VMEM = 42 << 20
SPLIT = 320


def dft_matrices():
    n = np.arange(SPAN)
    k = np.arange(BINS)
    angle = 2 * np.pi * ((k[:, None] * n[None, :]) % SPAN) / SPAN
    live = (k <= SPAN // 2)[:, None]
    forward = np.concatenate([np.cos(angle) * live, -np.sin(angle) * live], axis=0)
    weight = np.where((k == 0) | (k == SPAN // 2), 1.0, 2.0) * (k <= SPAN // 2) / SPAN
    back = np.concatenate(
        [np.cos(angle).T[TAPS:] * weight, -np.sin(angle).T[TAPS:] * weight], axis=1
    )
    return split_np(forward.astype(np.float32)), split_np(back.astype(np.float32))


def split_np(value):
    high = value.astype(jnp.bfloat16)
    low = (value - high.astype(np.float32)).astype(jnp.bfloat16)
    return np.stack([high, low])


def split(value):
    high = value.astype(jnp.bfloat16)
    return high, (value - high.astype(jnp.float32)).astype(jnp.bfloat16)


def mm(a, b):
    return jnp.dot(a, b, preferred_element_type=jnp.float32)


def mm_split(a, b):
    high, low = split(b)
    return mm(a[0], high) + (mm(a[0], low) + mm(a[1], high))


def slots_of(ids_row, axis):
    first = lax.broadcasted_iota(jnp.int32, (TOK, TOK), 0)
    second = lax.broadcasted_iota(jnp.int32, (TOK, TOK), 1)
    on_diagonal = jnp.where(first == second, ids_row.astype(jnp.float32), 0.0)
    ids_col = jnp.sum(on_diagonal, axis=1, keepdims=True).astype(jnp.int32)
    same = ids_col == ids_row
    earlier = (first < second) if axis == 0 else (second < first)
    rank = jnp.sum(jnp.where(same & earlier, 1.0, 0.0), axis=axis, keepdims=True)
    ids = ids_row if axis == 0 else ids_col
    return ids * CAP + rank.astype(jnp.int32)


def taps3(ext, filt, start, length):
    return (
        filt[0:1] * ext[start : start + length]
        + filt[1:2] * ext[start - 1 : start - 1 + length]
        + filt[2:3] * ext[start - 2 : start - 2 + length]
    )


def spectrum_kernel(proj, short, long_f, fwd, spec_out, filt_out, table, sem):
    copy = pltpu.make_async_copy(fwd, table, sem)

    @pl.when(pl.program_id(0) == 0)
    def _():
        copy.start()

    zeros = jnp.zeros((8, LANES), jnp.float32)

    def filtered(f):
        ext = jnp.concatenate([zeros, proj[f].astype(jnp.float32)], axis=0)
        return taps3(ext, short[f], 8, TOK)

    live = lax.broadcasted_iota(jnp.int32, (TOK, LANES), 0) >= 2
    kv = jnp.where(live, filtered(1) * filtered(2), 0.0).astype(jnp.bfloat16)

    @pl.when(pl.program_id(0) == 0)
    def _():
        copy.wait()

    filt_out[...] = mm_split((table[0, :, :TAPS], table[1, :, :TAPS]), long_f[...])
    spec_out[...] = mm(table[0, :, TAPS:], kv) + mm(table[1, :, TAPS:], kv)


def spectrum(projected, short, long_f, fwd):
    steps = QUARTER // LANES
    return pl.pallas_call(
        spectrum_kernel,
        grid=(steps,),
        in_specs=[
            pl.BlockSpec((3, TOK, LANES), lambda i: (0, 0, i)),
            pl.BlockSpec((3, 3, LANES), lambda i: (0, 0, i)),
            pl.BlockSpec((TAPS, LANES), lambda i: (0, i)),
            pl.BlockSpec(memory_space=pltpu.HBM),
        ],
        out_specs=[pl.BlockSpec((2 * BINS, LANES), lambda i: (0, i))] * 2,
        out_shape=[jax.ShapeDtypeStruct((2 * BINS, QUARTER), jnp.float32)] * 2,
        scratch_shapes=[
            pltpu.VMEM((2, 2 * BINS, SPAN), jnp.bfloat16),
            pltpu.SemaphoreType.DMA,
        ],
        compiler_params=pltpu.CompilerParams(vmem_limit_bytes=VMEM),
        cost_estimate=pl.CostEstimate(
            flops=4 << 30, bytes_accessed=8 << 20, transcendentals=0
        ),
        name="spectrum",
    )(projected, short, long_f, fwd)


def front_kernel(
    x_ref, proj, halo, short, spec, filt, res, gain, ids_row,
    fwd, back, h_out, send_out, fwd_table, back_table, sems,
):
    f32 = jnp.float32
    copies = [
        pltpu.make_async_copy(fwd, fwd_table, sems.at[0]),
        pltpu.make_async_copy(back, back_table, sems.at[1]),
    ]

    @pl.when(pl.program_id(0) == 0)
    def _():
        for copy in copies:
            copy.start()

    def filtered(f):
        ext = jnp.concatenate([halo[(f - 1) * HALO : f * HALO], proj[f, :QHALO]], axis=0).astype(f32)
        return taps3(ext, short[f], HALO - TAPS, HALO)

    live = lax.broadcasted_iota(jnp.int32, (HALO, LANES), 0) < TAPS + 2
    kv = jnp.where(live, filtered(1) * filtered(2), 0.0).astype(jnp.bfloat16)
    ext = jnp.concatenate([halo[2 * HALO :], proj[0]], axis=0).astype(f32)
    s0 = taps3(ext, short[0], QHALO, TOK)

    @pl.when(pl.program_id(0) == 0)
    def _():
        for copy in copies:
            copy.wait()

    total = spec[...] + mm(fwd_table[0, :, :HALO], kv) + mm(fwd_table[1, :, :HALO], kv)
    re, im = total[:BINS], total[BINS:]
    fre, fim = filt[:BINS], filt[BINS:]
    prod = jnp.concatenate([re * fre - im * fim, re * fim + im * fre], axis=0)
    long_out = mm_split((back_table[0], back_table[1]), prod)
    h = (res[...].astype(f32) + s0 * long_out).astype(jnp.bfloat16)
    h_out[...] = h
    gained = (h.astype(f32) * gain[...]).astype(jnp.bfloat16)
    slot_row = slots_of(ids_row[...], 0)
    slot = lax.broadcasted_iota(jnp.int32, (SLOTS, TOK), 0)
    pick = jnp.where(slot == slot_row, 1.0, 0.0).astype(jnp.bfloat16)
    send_out[...] = mm(pick, gained).astype(jnp.bfloat16)


def front(x_at, projected, halo, short, spec, filt, res, gain, ids, fwd, back):
    steps = QUARTER // LANES

    def whole(shape):
        return pl.BlockSpec(shape, lambda i, x: (0,) * len(shape))

    def columns(rows):
        return pl.BlockSpec((rows, LANES), lambda i, x: (0, i))

    return pl.pallas_call(
        front_kernel,
        grid_spec=pltpu.PrefetchScalarGridSpec(
            num_scalar_prefetch=1,
            grid=(steps,),
            in_specs=[
                pl.BlockSpec((3, TOK, LANES), lambda i, x: (0, 0, i)),
                columns(2 * HALO + QHALO),
                pl.BlockSpec((3, 3, LANES), lambda i, x: (0, 0, i)),
                columns(2 * BINS),
                columns(2 * BINS),
                columns(TOK),
                pl.BlockSpec((1, LANES), lambda i, x: (0, x[0] * steps + i)),
                whole((1, TOK)),
                pl.BlockSpec(memory_space=pltpu.HBM),
                pl.BlockSpec(memory_space=pltpu.HBM),
            ],
            out_specs=[columns(TOK), columns(SLOTS)],
            scratch_shapes=[
                pltpu.VMEM((2, 2 * BINS, SPAN), jnp.bfloat16),
                pltpu.VMEM((2, TOK, 2 * BINS), jnp.bfloat16),
                pltpu.SemaphoreType.DMA((2,)),
            ],
        ),
        out_shape=[
            jax.ShapeDtypeStruct((TOK, QUARTER), jnp.bfloat16),
            jax.ShapeDtypeStruct((SLOTS, QUARTER), jnp.bfloat16),
        ],
        compiler_params=pltpu.CompilerParams(vmem_limit_bytes=VMEM),
        name="front",
    )(
        x_at, projected, halo, short, spec, filt, res, gain.reshape(1, D),
        ids.reshape(1, TOK), fwd, back,
    )


K_OFFSET = (0, 3, 1, 2)
N_OFFSET = (2, 1, 3, 0)


def middle(rows):
    return (rows // 2 + 15) // 16 * 16


def aligned(q):
    return pl.ds(pl.multiple_of(q * QUARTER, QUARTER), QUARTER)


def x_copy(piece, xs, block, start, sem):
    return pltpu.make_async_copy(piece, xs.at[block, pl.ds(start, piece.shape[0])], sem)


def add_squares(squares, xk, ig):
    h = xk.astype(jnp.float32) * ig
    sq = h * h
    for c in range(QUARTER // 128):
        squares = squares + sq[:, c * 128 : (c + 1) * 128]
    return squares


def near_kernel(x_ref, *refs):
    pieces = refs[:6]
    wg, wu, ig, g_out, u_out, sq_out, xs, wgs, wus, accg, accu, x_sem, w_sem, y_sem = refs[6:]
    rows = accg.shape[0]
    half = rows // 2
    k_at = [lax.rem(x_ref[0] + K_OFFSET[k], 4) for k in range(3)]
    copies = []
    for k in range(3):
        copies.append(
            [
                x_copy(pieces[k], xs, k, 0, x_sem.at[k]),
                x_copy(pieces[3 + k], xs, k, half, x_sem.at[3 + k]),
                pltpu.make_async_copy(wg.at[aligned(k_at[k])], wgs.at[k], w_sem.at[0, k]),
                pltpu.make_async_copy(wu.at[aligned(k_at[k])], wus.at[k], w_sem.at[1, k]),
            ]
        )
        for copy in copies[k]:
            copy.start()
    squares = jnp.zeros((rows, 128), jnp.float32)
    for k in range(3):
        for copy in copies[k]:
            copy.wait()
        g = mm(xs[k], wgs[k])
        u = mm(xs[k], wus[k])
        squares = add_squares(squares, xs[k], ig[k_at[k]])
        if k == 0:
            accg[...] = g
            accu[...] = u
        else:
            accg[...] += g
            accu[...] += u
    sq_out[...] = squares
    outs = [
        pltpu.make_async_copy(accg, g_out, y_sem.at[0]),
        pltpu.make_async_copy(accu, u_out, y_sem.at[1]),
    ]
    for copy in outs:
        copy.start()
    for copy in outs:
        copy.wait()


def near(x_at, pieces, wg, wu, inv_gain):
    rows = 2 * pieces[0].shape[0]
    any_spec = pl.BlockSpec(memory_space=pl.ANY)
    vmem_spec = pl.BlockSpec(memory_space=pltpu.VMEM)
    bf16, f32 = jnp.bfloat16, jnp.float32
    return pl.pallas_call(
        near_kernel,
        in_specs=[pl.BlockSpec(memory_space=pltpu.SMEM)] + [any_spec] * 8 + [vmem_spec],
        out_specs=[any_spec, any_spec, vmem_spec],
        out_shape=[
            jax.ShapeDtypeStruct((rows, HID), f32),
            jax.ShapeDtypeStruct((rows, HID), f32),
            jax.ShapeDtypeStruct((rows, 128), f32),
        ],
        scratch_shapes=[
            pltpu.VMEM((3, rows, QUARTER), bf16),
            pltpu.VMEM((3, QUARTER, HID), bf16),
            pltpu.VMEM((3, QUARTER, HID), bf16),
            pltpu.VMEM((rows, HID), f32),
            pltpu.VMEM((rows, HID), f32),
            pltpu.SemaphoreType.DMA((6,)),
            pltpu.SemaphoreType.DMA((2, 3)),
            pltpu.SemaphoreType.DMA((2,)),
        ],
        compiler_params=pltpu.CompilerParams(vmem_limit_bytes=VMEM),
        cost_estimate=pl.CostEstimate(
            flops=0, bytes_accessed=0, transcendentals=0
        ),
        name="near",
    )(x_at, *pieces, wg, wu, inv_gain)


def far_kernel(x_ref, *refs):
    pieces = refs[:4]
    g_in, u_in, sq_in, wg, wu, wd, ig = refs[4:11]
    outs = refs[11:19]
    xs, wgs, wus, wds, ys, accg, accu, hid, x_sem, w_sem, a_sem, y_sem = refs[19:]
    rows = accg.shape[0]
    half = rows // 2
    mid = middle(half)
    spans = (mid, half - mid)
    k_at = lax.rem(x_ref[0] + K_OFFSET[3], 4)
    first = [
        x_copy(pieces[n], xs, 0, n // 2 * half + n % 2 * mid, x_sem.at[n]) for n in range(4)
    ] + [
        pltpu.make_async_copy(wg.at[aligned(k_at)], wgs, w_sem.at[0]),
        pltpu.make_async_copy(wu.at[aligned(k_at)], wus, w_sem.at[1]),
    ]
    sums = [
        pltpu.make_async_copy(g_in, accg, a_sem.at[0]),
        pltpu.make_async_copy(u_in, accu, a_sem.at[1]),
    ]
    down = [
        pltpu.make_async_copy(
            wd.at[:, aligned(lax.rem(x_ref[0] + N_OFFSET[j], 4))], wds.at[j], w_sem.at[2 + j]
        )
        for j in range(4)
    ]
    for copy in first + sums + down:
        copy.start()

    places = {
        (0, 0): (0, 0), (0, 1): (1, 1), (1, 0): (2, 0), (1, 1): (0, 1),
        (2, 0): (1, 0), (2, 1): (2, 1), (3, 0): (3, 0), (3, 1): (3, 1),
    }
    results = [[] for _ in range(4)]
    for (j, upper), (out, at) in places.items():
        for core in range(2):
            results[j].append(
                pltpu.make_async_copy(
                    ys.at[j, pl.ds(core * half + upper * mid, spans[upper])],
                    outs[core * 4 + out].at[pl.ds(at * mid, spans[upper])],
                    y_sem.at[j, core * 2 + upper],
                )
            )
    for copy in first:
        copy.wait()
    xk = xs[0]
    g = mm(xk, wgs[...])
    u = mm(xk, wus[...])
    squares = add_squares(sq_in[...], xk, ig[k_at])
    scale = lax.rsqrt(jnp.sum(squares, axis=1, keepdims=True) / D + 1e-06)
    for copy in sums:
        copy.wait()
    gate = (accg[...] + g) * scale
    up = (accu[...] + u) * scale
    hid[...] = (gate / (1.0 + jnp.exp(-gate)) * up).astype(jnp.bfloat16)
    for j in range(4):
        down[j].wait()
        ys[j] = mm(hid[...], wds[j]).astype(jnp.bfloat16)
        for copy in results[j]:
            copy.start()
    for j in range(4):
        for copy in results[j]:
            copy.wait()


def far(x_at, pieces, sums, wg, wu, wd, inv_gain):
    rows = sums[0].shape[0]
    any_spec = pl.BlockSpec(memory_space=pl.ANY)
    vmem_spec = pl.BlockSpec(memory_space=pltpu.VMEM)
    bf16, f32 = jnp.bfloat16, jnp.float32
    return pl.pallas_call(
        far_kernel,
        in_specs=[pl.BlockSpec(memory_space=pltpu.SMEM)]
        + [any_spec] * 6
        + [vmem_spec]
        + [any_spec] * 3
        + [vmem_spec],
        out_specs=[any_spec] * 8,
        out_shape=[jax.ShapeDtypeStruct((rows // 2, QUARTER), bf16)] * 8,
        scratch_shapes=[
            pltpu.VMEM((1, rows, QUARTER), bf16),
            pltpu.VMEM((QUARTER, HID), bf16),
            pltpu.VMEM((QUARTER, HID), bf16),
            pltpu.VMEM((4, HID, QUARTER), bf16),
            pltpu.VMEM((4, rows, QUARTER), bf16),
            pltpu.VMEM((rows, HID), f32),
            pltpu.VMEM((rows, HID), f32),
            pltpu.VMEM((rows, HID), bf16),
            pltpu.SemaphoreType.DMA((4,)),
            pltpu.SemaphoreType.DMA((6,)),
            pltpu.SemaphoreType.DMA((2,)),
            pltpu.SemaphoreType.DMA((4, 4)),
        ],
        compiler_params=pltpu.CompilerParams(vmem_limit_bytes=VMEM),
        cost_estimate=pl.CostEstimate(
            flops=0, bytes_accessed=0, transcendentals=0
        ),
        name="far",
    )(x_at, *pieces, *sums, wg, wu, wd, inv_gain)


def finish_kernel(h, back, ids_row, out):
    slot_col = slots_of(ids_row[...], 1)
    slot = lax.broadcasted_iota(jnp.int32, (TOK, SLOTS), 1)
    pick = jnp.where(slot == slot_col, 1.0, 0.0).astype(jnp.bfloat16)
    moe = mm(pick, back[...])
    out[...] = (h[...].astype(jnp.float32) + moe).astype(jnp.bfloat16)


def finish(h, back, ids):
    return pl.pallas_call(
        finish_kernel,
        grid=(QUARTER // LANES,),
        in_specs=[
            pl.BlockSpec((TOK, LANES), lambda i: (0, i)),
            pl.BlockSpec((SLOTS, LANES), lambda i: (0, i)),
            pl.BlockSpec((1, TOK), lambda i: (0, 0)),
        ],
        out_specs=pl.BlockSpec((TOK, LANES), lambda i: (0, i)),
        out_shape=jax.ShapeDtypeStruct((TOK, QUARTER), jnp.bfloat16),
        compiler_params=pltpu.CompilerParams(vmem_limit_bytes=VMEM),
        name="finish",
    )(h, back, ids.reshape(1, TOK))


def along_x(block, step):
    return lax.ppermute(block, "x", [(i, (i + step) % 4) for i in range(4)])


def other_core(block):
    return lax.ppermute(block, "c", [(0, 1), (1, 0)])


def add(*terms):
    total = terms[0].astype(jnp.float32)
    for term in terms[1:]:
        total = total + term.astype(jnp.float32)
    return total.astype(jnp.bfloat16)


def after(values, *earlier):
    return list(lax.optimization_barrier((tuple(values), earlier))[0])


def core_sums(outs):
    return [add(outs[j], other_core(outs[4 + j])) for j in range(4)]


def body(
    projected, short_filter, long_filter, residual_in, norm_gain, expert_ids,
    gate_weight, up_weight, down_weight,
):
    x_at = lax.axis_index("x").astype(jnp.int32).reshape(1)
    fwd, bck = (jnp.asarray(table) for table in dft_matrices())
    edge = jnp.concatenate(
        [projected[1, TOK - HALO :], projected[2, TOK - HALO :], projected[0, TOK - QHALO :]],
        axis=0,
    )
    halo = lax.ppermute(edge, ("z", "y", "c"), [(i, i + 1) for i in range(31)])
    spec, filt = spectrum(projected, short_filter, long_filter, fwd)
    h, send = front(
        x_at, projected, halo, short_filter, spec, filt, residual_in, norm_gain, expert_ids,
        fwd, bck,
    )
    got = lax.all_to_all(
        send.reshape(EXPERTS, CAP, QUARTER), ("z", "y"), split_axis=0, concat_axis=0, tiled=True
    ).reshape(SLOTS, QUARTER)
    inv_gain = (1.0 / norm_gain).reshape(4, 1, QUARTER)
    wg, wu, wd = gate_weight[0], up_weight[0], down_weight[0]

    def both_cores(pieces):
        return [*pieces, *(other_core(p) for p in pieces)]

    def forward(left, right):
        mid = middle(left.shape[0])
        return [along_x(left[:mid], 1), along_x(right[mid:], -1)]

    def second_wave(sums, to_right, to_left):
        mid = middle(to_right.shape[0])
        lower = along_x(add(sums[2][:mid], to_right[:mid]), 1)
        upper = along_x(add(sums[2][mid:], to_left[mid:]), -1)
        return [
            add(sums[3][:mid], lower, to_left[:mid]),
            add(sums[3][mid:], to_right[mid:], upper),
        ]

    own0, own1 = got[:SPLIT], got[SPLIT:]
    left0, right0 = along_x(own0, 1), along_x(own0, -1)
    (own1,) = after([own1], left0, right0)
    far0 = forward(left0, right0)
    left1, right1 = along_x(own1, 1), along_x(own1, -1)
    part0 = near(x_at, both_cores([own0, left0, right0]), wg, wu, inv_gain)
    far0 = after(far0, part0[2])
    outs0 = far(x_at, both_cores(far0), part0, wg, wu, wd, inv_gain)
    twin1 = other_core(own1)
    left1, right1 = after([left1, right1], outs0[0])
    far1 = forward(left1, right1)
    sums0 = core_sums(outs0)
    part1 = near(x_at, [own1, left1, right1, twin1, other_core(left1), other_core(right1)], wg, wu, inv_gain)
    far1 = after(far1, part1[2], *sums0[:2])
    wave0 = [along_x(sums0[0], 1), along_x(sums0[1], -1)]
    outs1 = far(x_at, both_cores(far1), part1, wg, wu, wd, inv_gain)
    wave0 = after(wave0, outs1[0])
    sums1 = core_sums(outs1)
    done0 = second_wave(sums0, *wave0)
    wave1 = [along_x(sums1[0], 1), along_x(sums1[1], -1)]
    done1 = second_wave(sums1, *wave1)
    back = lax.all_to_all(
        jnp.concatenate(done0 + done1, axis=0).reshape(EXPERTS, CAP, QUARTER),
        ("z", "y"), split_axis=0, concat_axis=0, tiled=True,
    ).reshape(SLOTS, QUARTER)
    return finish(h, back, expert_ids)


def solution(mesh):
    grid = Mesh(mesh.devices.reshape(4, 4, 2, 4), ("z", "y", "c", "x"))
    ctx = ("z", "y", "c")
    return jax.shard_map(
        body,
        mesh=grid,
        in_specs=(
            P(None, ctx, "x"),
            P(None, None, "x"),
            P(None, "x"),
            P(ctx, "x"),
            P(),
            P(ctx),
            P(ctx, None, "x"),
            P(ctx, None, "x"),
            P(ctx, "x", None),
        ),
        out_specs=P(ctx, "x"),
        check_vma=False,
    )
```

```python
import functools

import jax
import jax.numpy as jnp
import numpy as np
from jax import lax
from jax.experimental import pallas as pl
from jax.experimental.pallas import tpu as pltpu
from jax.sharding import Mesh
from jax.sharding import PartitionSpec as P

D = 4096
TAPS = 128
TOK = 256
QUARTER = 1024
HID = 768
EXPERTS = 16
CAP = 40
SLOTS = EXPERTS * CAP
SPAN = TOK + TAPS
BINS = 200
HALO = 144
QHALO = 16
LANES = 512
VMEM = 42 << 20
SPLIT = 320


def dft_matrices():
    n = np.arange(SPAN)
    k = np.arange(BINS)
    angle = 2 * np.pi * ((k[:, None] * n[None, :]) % SPAN) / SPAN
    live = (k <= SPAN // 2)[:, None]
    forward = np.concatenate([np.cos(angle) * live, -np.sin(angle) * live], axis=0)
    weight = np.where((k == 0) | (k == SPAN // 2), 1.0, 2.0) * (k <= SPAN // 2) / SPAN
    back = np.concatenate(
        [np.cos(angle).T[TAPS:] * weight, -np.sin(angle).T[TAPS:] * weight], axis=1
    )
    return split_np(forward.astype(np.float32)), split_np(back.astype(np.float32))


def split_np(value):
    high = value.astype(jnp.bfloat16)
    low = (value - high.astype(np.float32)).astype(jnp.bfloat16)
    return np.stack([high, low])


def split(value):
    high = value.astype(jnp.bfloat16)
    return high, (value - high.astype(jnp.float32)).astype(jnp.bfloat16)


def mm(a, b):
    return jnp.dot(a, b, preferred_element_type=jnp.float32)


def mm_split(a, b):
    high, low = split(b)
    return mm(a[0], high) + (mm(a[0], low) + mm(a[1], high))


def slots_of(ids_row, axis):
    first = lax.broadcasted_iota(jnp.int32, (TOK, TOK), 0)
    second = lax.broadcasted_iota(jnp.int32, (TOK, TOK), 1)
    on_diagonal = jnp.where(first == second, ids_row.astype(jnp.float32), 0.0)
    ids_col = jnp.sum(on_diagonal, axis=1, keepdims=True).astype(jnp.int32)
    same = ids_col == ids_row
    earlier = (first < second) if axis == 0 else (second < first)
    rank = jnp.sum(jnp.where(same & earlier, 1.0, 0.0), axis=axis, keepdims=True)
    ids = ids_row if axis == 0 else ids_col
    return ids * CAP + rank.astype(jnp.int32)


def taps3(ext, filt, start, length):
    return (
        filt[0:1] * ext[start : start + length]
        + filt[1:2] * ext[start - 1 : start - 1 + length]
        + filt[2:3] * ext[start - 2 : start - 2 + length]
    )


def spectrum_kernel(proj, short, long_f, fwd, spec_out, filt_out, table, sem):
    copy = pltpu.make_async_copy(fwd, table, sem)

    @pl.when(pl.program_id(0) == 0)
    def _():
        copy.start()

    zeros = jnp.zeros((8, LANES), jnp.float32)

    def filtered(f):
        ext = jnp.concatenate([zeros, proj[f].astype(jnp.float32)], axis=0)
        return taps3(ext, short[f], 8, TOK)

    live = lax.broadcasted_iota(jnp.int32, (TOK, LANES), 0) >= 2
    kv = jnp.where(live, filtered(1) * filtered(2), 0.0).astype(jnp.bfloat16)

    @pl.when(pl.program_id(0) == 0)
    def _():
        copy.wait()

    filt_out[...] = mm_split((table[0, :, :TAPS], table[1, :, :TAPS]), long_f[...])
    spec_out[...] = mm(table[0, :, TAPS:], kv) + mm(table[1, :, TAPS:], kv)


def spectrum(projected, short, long_f, fwd):
    steps = QUARTER // LANES
    return pl.pallas_call(
        spectrum_kernel,
        grid=(steps,),
        in_specs=[
            pl.BlockSpec((3, TOK, LANES), lambda i: (0, 0, i)),
            pl.BlockSpec((3, 3, LANES), lambda i: (0, 0, i)),
            pl.BlockSpec((TAPS, LANES), lambda i: (0, i)),
            pl.BlockSpec(memory_space=pltpu.HBM),
        ],
        out_specs=[pl.BlockSpec((2 * BINS, LANES), lambda i: (0, i))] * 2,
        out_shape=[jax.ShapeDtypeStruct((2 * BINS, QUARTER), jnp.float32)] * 2,
        scratch_shapes=[
            pltpu.VMEM((2, 2 * BINS, SPAN), jnp.bfloat16),
            pltpu.SemaphoreType.DMA,
        ],
        compiler_params=pltpu.CompilerParams(vmem_limit_bytes=VMEM),
        cost_estimate=pl.CostEstimate(
            flops=4 << 30, bytes_accessed=8 << 20, transcendentals=0
        ),
        name="spectrum",
    )(projected, short, long_f, fwd)


def front_kernel(
    x_ref, proj, halo, short, spec, filt, res, gain, ids_row,
    fwd, back, h_out, send_out, fwd_table, back_table, sems,
):
    f32 = jnp.float32
    copies = [
        pltpu.make_async_copy(fwd, fwd_table, sems.at[0]),
        pltpu.make_async_copy(back, back_table, sems.at[1]),
    ]

    @pl.when(pl.program_id(0) == 0)
    def _():
        for copy in copies:
            copy.start()

    def filtered(f):
        ext = jnp.concatenate([halo[(f - 1) * HALO : f * HALO], proj[f, :QHALO]], axis=0).astype(f32)
        return taps3(ext, short[f], HALO - TAPS, HALO)

    live = lax.broadcasted_iota(jnp.int32, (HALO, LANES), 0) < TAPS + 2
    kv = jnp.where(live, filtered(1) * filtered(2), 0.0).astype(jnp.bfloat16)
    ext = jnp.concatenate([halo[2 * HALO :], proj[0]], axis=0).astype(f32)
    s0 = taps3(ext, short[0], QHALO, TOK)

    @pl.when(pl.program_id(0) == 0)
    def _():
        for copy in copies:
            copy.wait()

    total = spec[...] + mm(fwd_table[0, :, :HALO], kv) + mm(fwd_table[1, :, :HALO], kv)
    re, im = total[:BINS], total[BINS:]
    fre, fim = filt[:BINS], filt[BINS:]
    prod = jnp.concatenate([re * fre - im * fim, re * fim + im * fre], axis=0)
    long_out = mm_split((back_table[0], back_table[1]), prod)
    h = (res[...].astype(f32) + s0 * long_out).astype(jnp.bfloat16)
    h_out[...] = h
    gained = (h.astype(f32) * gain[...]).astype(jnp.bfloat16)
    slot_row = slots_of(ids_row[...], 0)
    slot = lax.broadcasted_iota(jnp.int32, (SLOTS, TOK), 0)
    pick = jnp.where(slot == slot_row, 1.0, 0.0).astype(jnp.bfloat16)
    send_out[...] = mm(pick, gained).astype(jnp.bfloat16)


def front(x_at, projected, halo, short, spec, filt, res, gain, ids, fwd, back):
    steps = QUARTER // LANES

    def whole(shape):
        return pl.BlockSpec(shape, lambda i, x: (0,) * len(shape))

    def columns(rows):
        return pl.BlockSpec((rows, LANES), lambda i, x: (0, i))

    return pl.pallas_call(
        front_kernel,
        grid_spec=pltpu.PrefetchScalarGridSpec(
            num_scalar_prefetch=1,
            grid=(steps,),
            in_specs=[
                pl.BlockSpec((3, TOK, LANES), lambda i, x: (0, 0, i)),
                columns(2 * HALO + QHALO),
                pl.BlockSpec((3, 3, LANES), lambda i, x: (0, 0, i)),
                columns(2 * BINS),
                columns(2 * BINS),
                columns(TOK),
                pl.BlockSpec((1, LANES), lambda i, x: (0, x[0] * steps + i)),
                whole((1, TOK)),
                pl.BlockSpec(memory_space=pltpu.HBM),
                pl.BlockSpec(memory_space=pltpu.HBM),
            ],
            out_specs=[columns(TOK), columns(SLOTS)],
            scratch_shapes=[
                pltpu.VMEM((2, 2 * BINS, SPAN), jnp.bfloat16),
                pltpu.VMEM((2, TOK, 2 * BINS), jnp.bfloat16),
                pltpu.SemaphoreType.DMA((2,)),
            ],
        ),
        out_shape=[
            jax.ShapeDtypeStruct((TOK, QUARTER), jnp.bfloat16),
            jax.ShapeDtypeStruct((SLOTS, QUARTER), jnp.bfloat16),
        ],
        compiler_params=pltpu.CompilerParams(vmem_limit_bytes=VMEM),
        name="front",
    )(
        x_at, projected, halo, short, spec, filt, res, gain.reshape(1, D),
        ids.reshape(1, TOK), fwd, back,
    )


K_OFFSET = (0, 3, 1, 2)
N_OFFSET = (2, 1, 3, 0)


def middle(rows):
    return (rows // 2 + 15) // 16 * 16


def aligned(q):
    return pl.ds(pl.multiple_of(q * QUARTER, QUARTER), QUARTER)


def x_copy(piece, xs, block, start, sem):
    return pltpu.make_async_copy(piece, xs.at[block, pl.ds(start, piece.shape[0])], sem)


def add_squares(squares, xk, ig):
    h = xk.astype(jnp.float32) * ig
    sq = h * h
    for c in range(QUARTER // 128):
        squares = squares + sq[:, c * 128 : (c + 1) * 128]
    return squares


def near_kernel(blocks, earlier, x_ref, *refs):
    count = len(blocks)
    pieces, refs = refs[: 2 * count], refs[2 * count :]
    before, refs = refs[: 3 * earlier], refs[3 * earlier :]
    wg, wu, ig, g_out, u_out, sq_out, xs, wgs, wus, accg, accu, x_sem, w_sem, a_sem, y_sem = refs
    rows = accg.shape[0]
    half = rows // 2
    k_at = [lax.rem(x_ref[0] + K_OFFSET[block], 4) for block in blocks]
    copies = []
    for k in range(count):
        copies.append(
            [
                x_copy(pieces[k], xs, k, 0, x_sem.at[k]),
                x_copy(pieces[count + k], xs, k, half, x_sem.at[count + k]),
                pltpu.make_async_copy(wg.at[aligned(k_at[k])], wgs.at[k], w_sem.at[0, k]),
                pltpu.make_async_copy(wu.at[aligned(k_at[k])], wus.at[k], w_sem.at[1, k]),
            ]
        )
    sums = [
        pltpu.make_async_copy(total, acc, a_sem.at[n])
        for n, (total, acc) in enumerate(zip(before[:2], (accg, accu)))
    ]
    outs = [
        pltpu.make_async_copy(accg, g_out, y_sem.at[0]),
        pltpu.make_async_copy(accu, u_out, y_sem.at[1]),
    ]
    for copy in copies[0] + sums:
        copy.start()
    for k in range(1, count):
        for copy in copies[k]:
            copy.start()
    squares = before[2][...] if earlier else jnp.zeros((rows, 128), jnp.float32)
    for k in range(count):
        for copy in copies[k][:2]:
            copy.wait()
        for n, (weight, acc) in enumerate(((wgs, accg), (wus, accu))):
            copies[k][2 + n].wait()
            product = mm(xs[k], weight[k])
            if k == 0 and earlier:
                sums[n].wait()
            if k == 0 and not earlier:
                acc[...] = product
            else:
                acc[...] += product
            if k == count - 1:
                outs[n].start()
        squares = add_squares(squares, xs[k], ig[k_at[k]])
    sq_out[...] = squares
    for copy in outs:
        copy.wait()


def near(x_at, blocks, pieces, sums, wg, wu, inv_gain):
    rows = 2 * pieces[0].shape[0]
    count = len(blocks)
    any_spec = pl.BlockSpec(memory_space=pl.ANY)
    vmem_spec = pl.BlockSpec(memory_space=pltpu.VMEM)
    bf16, f32 = jnp.bfloat16, jnp.float32
    sum_specs = [any_spec, any_spec, vmem_spec]
    return pl.pallas_call(
        functools.partial(near_kernel, blocks, len(sums) > 0),
        in_specs=[pl.BlockSpec(memory_space=pltpu.SMEM)]
        + [any_spec] * (2 * count)
        + sum_specs[: len(sums)]
        + [any_spec] * 2
        + [vmem_spec],
        out_specs=sum_specs,
        out_shape=[
            jax.ShapeDtypeStruct((rows, HID), f32),
            jax.ShapeDtypeStruct((rows, HID), f32),
            jax.ShapeDtypeStruct((rows, 128), f32),
        ],
        scratch_shapes=[
            pltpu.VMEM((count, rows, QUARTER), bf16),
            pltpu.VMEM((count, QUARTER, HID), bf16),
            pltpu.VMEM((count, QUARTER, HID), bf16),
            pltpu.VMEM((rows, HID), f32),
            pltpu.VMEM((rows, HID), f32),
            pltpu.SemaphoreType.DMA((2 * count,)),
            pltpu.SemaphoreType.DMA((2, count)),
            pltpu.SemaphoreType.DMA((2,)),
            pltpu.SemaphoreType.DMA((2,)),
        ],
        compiler_params=pltpu.CompilerParams(vmem_limit_bytes=VMEM),
        cost_estimate=pl.CostEstimate(flops=0, bytes_accessed=0, transcendentals=0),
        name="near" if sums else "first",
    )(x_at, *pieces, *sums, wg, wu, inv_gain)


def far_kernel(x_ref, *refs):
    pieces = refs[:4]
    g_in, u_in, sq_in, wg, wu, wd, ig = refs[4:11]
    outs = refs[11:19]
    xs, wgs, wus, wds, ys, accg, accu, hid, x_sem, w_sem, a_sem, y_sem = refs[19:]
    rows = accg.shape[0]
    half = rows // 2
    mid = middle(half)
    spans = (mid, half - mid)
    k_at = lax.rem(x_ref[0] + K_OFFSET[3], 4)
    first = [
        x_copy(pieces[n], xs, 0, n // 2 * half + n % 2 * mid, x_sem.at[n]) for n in range(4)
    ] + [
        pltpu.make_async_copy(wg.at[aligned(k_at)], wgs, w_sem.at[0]),
        pltpu.make_async_copy(wu.at[aligned(k_at)], wus, w_sem.at[1]),
    ]
    sums = [
        pltpu.make_async_copy(g_in, accg, a_sem.at[0]),
        pltpu.make_async_copy(u_in, accu, a_sem.at[1]),
    ]
    down = [
        pltpu.make_async_copy(
            wd.at[:, aligned(lax.rem(x_ref[0] + N_OFFSET[j], 4))], wds.at[j], w_sem.at[2 + j]
        )
        for j in range(4)
    ]
    for copy in first + sums + down:
        copy.start()

    places = {
        (0, 0): (0, 0), (0, 1): (1, 1), (1, 0): (2, 0), (1, 1): (0, 1),
        (2, 0): (1, 0), (2, 1): (2, 1), (3, 0): (3, 0), (3, 1): (3, 1),
    }
    results = [[] for _ in range(4)]
    for (j, upper), (out, at) in places.items():
        for core in range(2):
            results[j].append(
                pltpu.make_async_copy(
                    ys.at[j, pl.ds(core * half + upper * mid, spans[upper])],
                    outs[core * 4 + out].at[pl.ds(at * mid, spans[upper])],
                    y_sem.at[j, core * 2 + upper],
                )
            )
    for copy in first[:5]:
        copy.wait()
    xk = xs[0]
    g = mm(xk, wgs[...])
    first[5].wait()
    u = mm(xk, wus[...])
    squares = add_squares(sq_in[...], xk, ig[k_at])
    scale = lax.rsqrt(jnp.sum(squares, axis=1, keepdims=True) / D + 1e-06)
    for copy in sums:
        copy.wait()
    gate = (accg[...] + g) * scale
    up = (accu[...] + u) * scale
    hid[...] = (gate / (1.0 + jnp.exp(-gate)) * up).astype(jnp.bfloat16)
    for j in range(4):
        down[j].wait()
        ys[j] = mm(hid[...], wds[j]).astype(jnp.bfloat16)
        for copy in results[j]:
            copy.start()
    for j in range(4):
        for copy in results[j]:
            copy.wait()


def far(x_at, pieces, sums, wg, wu, wd, inv_gain):
    rows = sums[0].shape[0]
    any_spec = pl.BlockSpec(memory_space=pl.ANY)
    vmem_spec = pl.BlockSpec(memory_space=pltpu.VMEM)
    bf16, f32 = jnp.bfloat16, jnp.float32
    return pl.pallas_call(
        far_kernel,
        in_specs=[pl.BlockSpec(memory_space=pltpu.SMEM)]
        + [any_spec] * 6
        + [vmem_spec]
        + [any_spec] * 3
        + [vmem_spec],
        out_specs=[any_spec] * 8,
        out_shape=[jax.ShapeDtypeStruct((rows // 2, QUARTER), bf16)] * 8,
        scratch_shapes=[
            pltpu.VMEM((1, rows, QUARTER), bf16),
            pltpu.VMEM((QUARTER, HID), bf16),
            pltpu.VMEM((QUARTER, HID), bf16),
            pltpu.VMEM((4, HID, QUARTER), bf16),
            pltpu.VMEM((4, rows, QUARTER), bf16),
            pltpu.VMEM((rows, HID), f32),
            pltpu.VMEM((rows, HID), f32),
            pltpu.VMEM((rows, HID), bf16),
            pltpu.SemaphoreType.DMA((4,)),
            pltpu.SemaphoreType.DMA((6,)),
            pltpu.SemaphoreType.DMA((2,)),
            pltpu.SemaphoreType.DMA((4, 4)),
        ],
        compiler_params=pltpu.CompilerParams(vmem_limit_bytes=VMEM),
        cost_estimate=pl.CostEstimate(
            flops=0, bytes_accessed=0, transcendentals=0
        ),
        name="far",
    )(x_at, *pieces, *sums, wg, wu, wd, inv_gain)


def finish_kernel(h, back, ids_row, out):
    slot_col = slots_of(ids_row[...], 1)
    slot = lax.broadcasted_iota(jnp.int32, (TOK, SLOTS), 1)
    pick = jnp.where(slot == slot_col, 1.0, 0.0).astype(jnp.bfloat16)
    moe = mm(pick, back[...])
    out[...] = (h[...].astype(jnp.float32) + moe).astype(jnp.bfloat16)


def finish(h, back, ids):
    return pl.pallas_call(
        finish_kernel,
        grid=(QUARTER // LANES,),
        in_specs=[
            pl.BlockSpec((TOK, LANES), lambda i: (0, i)),
            pl.BlockSpec((SLOTS, LANES), lambda i: (0, i)),
            pl.BlockSpec((1, TOK), lambda i: (0, 0)),
        ],
        out_specs=pl.BlockSpec((TOK, LANES), lambda i: (0, i)),
        out_shape=jax.ShapeDtypeStruct((TOK, QUARTER), jnp.bfloat16),
        compiler_params=pltpu.CompilerParams(vmem_limit_bytes=VMEM),
        name="finish",
    )(h, back, ids.reshape(1, TOK))


def along_x(block, step):
    return lax.ppermute(block, "x", [(i, (i + step) % 4) for i in range(4)])


def other_core(block):
    return lax.ppermute(block, "c", [(0, 1), (1, 0)])


def add(*terms):
    total = terms[0].astype(jnp.float32)
    for term in terms[1:]:
        total = total + term.astype(jnp.float32)
    return total.astype(jnp.bfloat16)


def after(values, *earlier):
    return list(lax.optimization_barrier((tuple(values), earlier))[0])


def core_sums(outs):
    return [add(outs[j], other_core(outs[4 + j])) for j in range(4)]


def body(
    projected, short_filter, long_filter, residual_in, norm_gain, expert_ids,
    gate_weight, up_weight, down_weight,
):
    x_at = lax.axis_index("x").astype(jnp.int32).reshape(1)
    fwd, bck = (jnp.asarray(table) for table in dft_matrices())
    edge = jnp.concatenate(
        [projected[1, TOK - HALO :], projected[2, TOK - HALO :], projected[0, TOK - QHALO :]],
        axis=0,
    )
    halo = lax.ppermute(edge, ("z", "y", "c"), [(i, i + 1) for i in range(31)])
    spec, filt = spectrum(projected, short_filter, long_filter, fwd)
    h, send = front(
        x_at, projected, halo, short_filter, spec, filt, residual_in, norm_gain, expert_ids,
        fwd, bck,
    )
    got = lax.all_to_all(
        send.reshape(EXPERTS, CAP, QUARTER), ("z", "y"), split_axis=0, concat_axis=0, tiled=True
    ).reshape(SLOTS, QUARTER)
    inv_gain = (1.0 / norm_gain).reshape(4, 1, QUARTER)
    wg, wu, wd = gate_weight[0], up_weight[0], down_weight[0]

    def both_cores(pieces):
        return [*pieces, *(other_core(p) for p in pieces)]

    def forward(left, right):
        mid = middle(left.shape[0])
        return [along_x(left[:mid], 1), along_x(right[mid:], -1)]

    def second_wave(sums, to_right, to_left):
        mid = middle(to_right.shape[0])
        lower = along_x(add(sums[2][:mid], to_right[:mid]), 1)
        upper = along_x(add(sums[2][mid:], to_left[mid:]), -1)
        return [
            add(sums[3][:mid], lower, to_left[:mid]),
            add(sums[3][mid:], to_right[mid:], upper),
        ]

    own0, own1 = got[:SPLIT], got[SPLIT:]
    left0, right0 = along_x(own0, 1), along_x(own0, -1)
    twin0, twin1 = other_core(own0), other_core(own1)
    first0 = near(x_at, (0,), [own0, twin0], (), wg, wu, inv_gain)
    left0, right0 = after([left0, right0], first0[2])
    (own1,) = after([own1], left0, right0)
    far0 = forward(left0, right0)
    left1, right1 = along_x(own1, 1), along_x(own1, -1)
    part0 = near(x_at, (1, 2), both_cores([left0, right0]), first0, wg, wu, inv_gain)
    far0 = after(far0, part0[2])
    outs0 = far(x_at, both_cores(far0), part0, wg, wu, wd, inv_gain)
    left1, right1 = after([left1, right1], outs0[0])
    far1 = forward(left1, right1)
    sums0 = core_sums(outs0)
    part1 = near(x_at, (0, 1, 2), [own1, left1, right1, twin1, other_core(left1), other_core(right1)], (), wg, wu, inv_gain)
    far1 = after(far1, part1[2], *sums0[:2])
    wave0 = [along_x(sums0[0], 1), along_x(sums0[1], -1)]
    outs1 = far(x_at, both_cores(far1), part1, wg, wu, wd, inv_gain)
    wave0 = after(wave0, outs1[0])
    sums1 = core_sums(outs1)
    done0 = second_wave(sums0, *wave0)
    wave1 = [along_x(sums1[0], 1), along_x(sums1[1], -1)]
    done1 = second_wave(sums1, *wave1)
    back = lax.all_to_all(
        jnp.concatenate(done0 + done1, axis=0).reshape(EXPERTS, CAP, QUARTER),
        ("z", "y"), split_axis=0, concat_axis=0, tiled=True,
    ).reshape(SLOTS, QUARTER)
    return finish(h, back, expert_ids)


def solution(mesh):
    grid = Mesh(mesh.devices.reshape(4, 4, 2, 4), ("z", "y", "c", "x"))
    ctx = ("z", "y", "c")
    return jax.shard_map(
        body,
        mesh=grid,
        in_specs=(
            P(None, ctx, "x"),
            P(None, None, "x"),
            P(None, "x"),
            P(ctx, "x"),
            P(),
            P(ctx),
            P(ctx, None, "x"),
            P(ctx, None, "x"),
            P(ctx, "x", None),
        ),
        out_specs=P(ctx, "x"),
        check_vma=False,
    )
```
